32 devices in a mesh: gx: 2 (over y), gy: 4 (over x, core), dir: 4 (over z).
Axes of the slice: x: 2, y: 2, z: 4, core: 2. Of those that a mesh axis runs over, the one named last changes fastest.
Arguments:
- directions: float32 [32, 256, 1024], P('dir', 'gx', 'gy'), may hold values from -6 to 6
- velocity: float32 [2, 256, 1024], P(None, 'gx', 'gy'), may hold values from -6 to 6
- viscosity: float32 [256, 1024], P('gx', 'gy'), may hold values from 0.5 to 2
- basal_drag: float32 [256, 1024], P('gx', 'gy'), may hold values from 0.5 to 8
- misfit_weight: float32 [256, 1024], P('gx', 'gy'), may hold values from 1 to 10
- ice_mask: int32 [256, 1024], P('gx', 'gy'), may hold values 0 or 1
- grounded: int32 [256, 1024], P('gx', 'gy'), may hold values 0 or 1
Outputs:
- basis: float32 [32, 256, 1024], P('dir', 'gx', 'gy')
- upper: float32 [32, 32], replicated
The draws below stay inside these ranges and needn't reach their ends.
All inputs are finite; a program needn't handle non-finite values. No bound on the sum of `ice_mask` or of `grounded` on one device may be relied on, other than what follows from the above.
Results may differ from the reference program's by a relative error of at most 0.00021.
Values sent between devices are 32-bit elements; how exact they have to be, the bound alone decides.
No kernel may reach another device: no remote copies, remote signals or barrier semaphores. Data moves between devices by JAX's collectives and lax.ppermute only.
A program may use at most 64 MiB of HBM per device.

```python
import math
import jax
import jax.numpy as jnp
from jax import lax

K = 32
SWEEPS = 6
NX = 256
NY = 1024


def place_ends(values, own_key, smallest, high):
    shape = values.shape
    spot = [jax.random.randint(jax.random.fold_in(own_key, axis), (), 0, shape[axis]) for axis in range(len(shape))]
    values = values.at[tuple(spot)].set(smallest)
    longest = shape.index(max(shape))
    spot[longest] = (spot[longest] + 1) % shape[longest]
    return values.at[tuple(spot)].set(high)


def block_scale(rng, extent, cuts, smallest, high):
    gain = 1.0
    for position, shards_of in cuts:
        heights = jax.random.uniform(jax.random.fold_in(jax.random.fold_in(rng, 6), position), (shards_of,), jnp.float32, smallest / len(cuts), high / len(cuts))
        gain = gain * jnp.repeat(jnp.exp(heights), extent[position] // shards_of).reshape((-1,) + (1,) * (len(extent) - 1 - position))
    return gain


def scatter_about(rng, extent, deviation, most, cuts=(), kind=jnp.bfloat16):
    values = deviation * jax.random.normal(rng, extent, jnp.float32)
    if cuts:
        values = values * block_scale(rng, extent, cuts, -0.22, 0.18)
    return jnp.clip(values, -most, most).astype(kind)


def setup_inputs(seed: int = 0) -> dict:
    key_of = jax.random.split(jax.random.key(seed), 8)
    directions = scatter_about(key_of[0], (K, NX, NY), 1.0, 6.0, ((0, 4), (1, 2), (2, 4)), jnp.float32)
    velocity = scatter_about(key_of[1], (2, NX, NY), 1.0, 6.0, ((1, 2), (2, 4)), jnp.float32)
    viscosity = jnp.clip(jnp.exp(math.log(2.0) - 1.3862944 * jax.random.uniform(key_of[2], (NX, NY), jnp.float32) ** block_scale(key_of[2], (NX, NY), ((0, 2), (1, 4)), -0.2, 0.2)), 0.5, 2.0)
    basal_drag = jnp.clip(jnp.exp(math.log(8.0) - 2.7725887 * jax.random.uniform(key_of[3], (NX, NY), jnp.float32) ** block_scale(key_of[3], (NX, NY), ((0, 2), (1, 4)), -0.2, 0.2)), 0.5, 8.0)
    misfit_weight = jnp.clip(jnp.exp(math.log(10.0) - 2.3025851 * jax.random.uniform(key_of[4], (NX, NY), jnp.float32) ** block_scale(key_of[4], (NX, NY), ((0, 2), (1, 4)), -0.2, 0.2)), 1.0, 10.0)
    ice_mask = place_ends((jax.random.randint(key_of[5], (NX, NY), 0, 16) < 15).astype(jnp.int32), jax.random.fold_in(key_of[5], 1), 0, 1)
    grounded = place_ends((jax.random.randint(key_of[6], (NX, NY), 0, 2) < 1).astype(jnp.int32), jax.random.fold_in(key_of[6], 1), 0, 1)
    return {"directions": directions, "velocity": velocity, "viscosity": viscosity, "basal_drag": basal_drag, "misfit_weight": misfit_weight, "ice_mask": ice_mask, "grounded": grounded}


damping = 0.8

def face_terms(viscosity):
    padded = jnp.pad(viscosity, 1)
    face_east = 0.5 * (viscosity + padded[2:, 1:-1])
    face_west = 0.5 * (viscosity + padded[:-2, 1:-1])
    face_north = 0.5 * (viscosity + padded[1:-1, 2:])
    face_south = 0.5 * (viscosity + padded[1:-1, :-2])
    return (face_east, face_west, face_north, face_south)

def weights_pair():
    along_x = jnp.array([4.0, 1.0], jnp.float32).reshape(2, 1, 1)
    along_y = jnp.array([1.0, 4.0], jnp.float32).reshape(2, 1, 1)
    return (along_x, along_y)

def relax_sweep(state, padded, coeffs, source):
    face_east, face_west, face_north, face_south, friction, diagonal, ice_keep = coeffs
    along_x, along_y = weights_pair()
    next_row = padded[..., 2:, 1:-1]
    prev_row = padded[..., :-2, 1:-1]
    next_col = padded[..., 1:-1, 2:]
    prev_col = padded[..., 1:-1, :-2]
    applied = along_x * (face_east * (state - next_row) + face_west * (state - prev_row))
    applied = applied + along_y * (face_north * (state - next_col) + face_south * (state - prev_col))
    applied = applied + friction * state
    return ice_keep * (state + damping * (source - applied) / diagonal)

def solve_field(source, coeffs):
    diagonal, ice_keep = (coeffs[5], coeffs[6])
    state = ice_keep * damping * source / diagonal
    for sweep in range(SWEEPS - 1):
        padded = jnp.pad(state, ((0, 0), (1, 1), (1, 1)))
        state = relax_sweep(state, padded, coeffs, source)
    return state

def reference(directions, velocity, viscosity, basal_drag, misfit_weight, ice_mask, grounded):
    face_east, face_west, face_north, face_south = face_terms(viscosity)
    friction = basal_drag * grounded.astype(jnp.float32)
    ice_keep = ice_mask.astype(jnp.float32)
    along_x, along_y = weights_pair()
    diagonal = along_x * (face_east + face_west) + along_y * (face_north + face_south) + friction
    coeffs = (face_east, face_west, face_north, face_south, friction, diagonal, ice_keep)

    def one_direction(direction):
        forward = solve_field(-friction * velocity * direction, coeffs)
        adjoint = solve_field(misfit_weight * forward, coeffs)
        return -friction * jnp.sum(velocity * adjoint, axis=0)
    sketch = lax.map(one_direction, directions)
    flat = sketch.reshape(K, NX * NY)
    gram = jnp.dot(flat.astype(jnp.float32), flat.T.astype(jnp.float32), precision=lax.Precision.HIGHEST, preferred_element_type=jnp.float32)
    gram = gram / jnp.float32(NX * NY)
    lower = jnp.linalg.cholesky(gram)
    inverse = lax.linalg.triangular_solve(lower, jnp.eye(K, dtype=jnp.float32), left_side=True, lower=True)
    basis = jnp.dot(inverse.astype(jnp.float32), flat.astype(jnp.float32), precision=lax.Precision.HIGHEST, preferred_element_type=jnp.float32)
    return (basis.reshape(K, NX, NY), lower.T)
```

```python
import functools

import jax
import jax.numpy as jnp
from jax import lax
from jax.experimental import pallas as pl
from jax.experimental.pallas import tpu as pltpu
from jax.sharding import PartitionSpec as P

SWEEPS = 6
damping = 0.8
KEEP_BACK = 1.0 - damping
REACH = 2 * (SWEEPS - 1)
PAD = 16
EDGE = REACH + 1
LANES = 128
STRIP = 32
PER = 12
F32 = jnp.float32
AXES = ("gx", "gy", "dir")
WEIGHTS = ((4.0, 1.0), (1.0, 4.0))


def lanes_of(shape):
    return lax.broadcasted_iota(jnp.int32, shape, len(shape) - 1)


def roll(value, shift, axis):
    size = value.shape[axis]
    return pltpu.roll(value, shift % size, axis)


def cell_fields(velocity, viscosity, drag, weight, mask, grounded, rows):
    friction = drag[rows, :] * grounded[rows, :].astype(F32)
    return (
        friction * velocity[0, rows, :],
        friction * velocity[1, rows, :],
        friction,
        viscosity[rows, :],
        weight[rows, :] * mask[rows, :].astype(F32),
    )


def pack_rows(place, dirs, velocity, viscosity, drag, weight, mask, grounded, *outs):
    rows = dirs.shape[1]
    for pairing, out in enumerate(outs):
        send_last = place[0] % 2 == pairing
        base = pl.multiple_of(jnp.where(send_last, rows - PAD, 0), PAD)
        turned = jnp.swapaxes(dirs[:, pl.ds(base, PAD), :], 0, 1)
        for j in range(REACH):
            out[j] = jnp.where(send_last, turned[PAD - REACH + j], turned[j])
        fields = cell_fields(
            velocity, viscosity, drag, weight, mask, grounded, pl.ds(base, PAD)
        )
        for k, field in enumerate(fields):
            for half in range(PAD // 8):
                out[REACH + (PAD // 8) * k + half] = field[8 * half : 8 * half + 8]


def extend(pairs_x, place, *refs):
    got, refs = refs[:pairs_x], refs[pairs_x:]
    dirs, velocity, viscosity, drag, weight, mask, grounded = refs[:7]
    dirs_ext, cells_ext, *outs = refs[7:]
    rows, cols = dirs.shape[1:]
    even = place[0] % 2 == 0

    def halo(i):
        one = got[0][i]
        two = got[1][i] if pairs_x > 1 else jnp.zeros_like(one)
        return jnp.where(even, two, one), jnp.where(even, one, two)

    for j in range(REACH):
        dirs_ext[PAD - REACH + j], dirs_ext[PAD + rows + j] = halo(j)
    for c in range(rows // 8):
        dirs_ext[PAD + 8 * c : PAD + 8 * c + 8] = jnp.swapaxes(
            dirs[:, 8 * c : 8 * c + 8, :], 0, 1
        )
    groups = PAD // 8
    for k in range(5):
        for half in range(groups):
            top, bottom = halo(REACH + groups * k + half)
            cells_ext[k, half] = top
            cells_ext[k, groups + rows // 8 + half] = bottom
    for c in range(rows // 8):
        fields = cell_fields(
            velocity, viscosity, drag, weight, mask, grounded, slice(8 * c, 8 * c + 8)
        )
        for k, field in enumerate(fields):
            cells_ext[k, groups + c] = field

    lane = lanes_of((8, LANES))
    tall = rows + 2 * REACH
    for pairing, out in enumerate(outs):
        send_last = place[1] % 2 == pairing
        turn = jnp.where(send_last, 1, 0)
        tile = pl.ds(pl.multiple_of(turn * (cols - LANES), LANES), LANES)

        def pick(value, k, width):
            shift = REACH * k + turn * width
            shift = jnp.where(shift >= LANES, shift - LANES, shift)
            inside = (lane >= REACH * k) & (lane < REACH * k + width)
            return inside, pltpu.roll(value, shift, 1)

        def group(g, count):
            held = jnp.zeros((8, LANES), F32)
            for j in range(count):
                inside, moved = pick(dirs_ext[PAD - REACH + PER * g + j, :, tile], j, REACH)
                held = jnp.where(inside, moved, held)
            out[g] = held

        def full(g, _):
            group(g, PER)
            return 0

        lax.fori_loop(0, tall // PER, full, 0)
        if tall % PER:
            group(tall // PER, tall % PER)
        first = pl.cdiv(tall, PER)

        def cell_group(g, _):
            held = jnp.zeros((8, LANES), F32)
            for k, field in enumerate((0, 1, 2, 4, 3)):
                width = EDGE if k == 4 else REACH
                inside, moved = pick(cells_ext[field, g, :, tile], k, width)
                held = jnp.where(inside, moved, held)
            out[first + g] = held
            return 0

        lax.fori_loop(0, cells_ext.shape[1], cell_group, 0)


def put_coeffs(out, comp, viscosity, south_of, north_of, friction, weight, pull, along_x, along_y):
    size = viscosity.shape[0]
    east = 0.5 * (viscosity + roll(viscosity, size - 1, 0))
    west = 0.5 * (viscosity + roll(viscosity, 1, 0))
    north = 0.5 * (viscosity + north_of)
    south = 0.5 * (viscosity + south_of)
    diagonal = along_x * (east + west) + along_y * (north + south) + friction
    step = jnp.where(weight != 0.0, damping / diagonal, 0.0)
    shape = (size // 8, 8, viscosity.shape[1])
    values = (
        step * along_x * east,
        step * along_x * west,
        step * along_y * north,
        step * along_y * south,
        -step * pull,
        step * weight,
    )
    for i, value in enumerate(values):
        out[comp, i] = value.reshape(shape)


def relax(comps, coeffs, base, ping, pong, rows, store):
    def sweep(source, put, first, last, extra=()):
        def one_row(c, j, held):
            states = []
            for m in range(comps):
                above, mid, below = held[m]
                e, w, n, s = (coeffs[m, i, c, j : j + 1, :] for i in range(4))
                states.append(
                    (base[m, 8 * c + j] + KEEP_BACK * mid)
                    + (e * below + w * above)
                    + (n * roll(mid, -1, 1) + s * roll(mid, 1, 1))
                )
            put(c, j, states)

        def chunk(c, _):
            held = [[source[m, 8 * c + j] for j in range(-1, 9)] for m in range(comps)]
            for j in range(8):
                one_row(c, j, [held[m][j : j + 3] for m in range(comps)])
            return 0

        for c, j in extra:
            row = 8 * c + j
            one_row(c, j, [[source[m, row + d] for d in (-1, 0, 1)] for m in range(comps)])
        lax.fori_loop(first, last, chunk, 0)

    lowest, highest = (PAD // 8 - 1, PAD // 8 + rows // 8 + 1)

    def to(ref):
        def put(c, j, states):
            for m in range(comps):
                ref[m, 8 * c + j] = states[m]

        return put

    def to_adjoint(c, j, states):
        for m in range(comps):
            base[m, 8 * c + j] = coeffs[m, 5, c, j : j + 1, :] * states[m]

    for solve in range(2):
        source = base
        for step in range(SWEEPS - 1):
            end = step == SWEEPS - 2
            target = ping if source is not ping else pong
            extra = ((lowest - 1, 7), (highest, 0)) if solve == 0 and step == 0 else ()
            if not end:
                sweep(source, to(target), lowest, highest, extra)
            elif solve == 0:
                sweep(source, to_adjoint, lowest, highest)
            else:
                sweep(source, store, lowest + 1, highest - 1)
            source = target


def solve_inner(dirs_ext, cells_ext, out, coeffs, base, ping, pong):
    rows, _, cols = out.shape
    size = rows + 2 * PAD
    viscosity = cells_ext[3].reshape(size, cols)
    friction = cells_ext[2].reshape(size, cols)
    weight = cells_ext[4].reshape(size, cols)
    for m in range(2):
        put_coeffs(
            coeffs,
            m,
            viscosity,
            roll(viscosity, 1, 1),
            roll(viscosity, -1, 1),
            friction,
            weight,
            cells_ext[m].reshape(size, cols),
            *WEIGHTS[m],
        )

    def start(c, j):
        for m in range(2):
            base[m, 8 * c + j] = coeffs[m, 4, c, j : j + 1, :] * dirs_ext[8 * c + j]

    def start_chunk(c, _):
        for j in range(8):
            start(c, j)
        return 0

    lax.fori_loop(PAD // 8 - 1, PAD // 8 + rows // 8 + 1, start_chunk, 0)
    for d in range(8, REACH):
        start(PAD // 8 - 2, 15 - d)
        start(PAD // 8 + rows // 8 + 1, d - 8)

    def store(c, j, states):
        pull = [cells_ext[m, c, j : j + 1, :] for m in range(2)]
        out[8 * c + j - PAD] = -(pull[0] * states[0] + pull[1] * states[1])

    relax(2, coeffs, base, ping, pong, rows, store)


def solve_edges(pairs_y, place, *refs):
    got, refs = refs[:pairs_y], refs[pairs_y:]
    dirs_ext, cells_ext, inner = refs[:3]
    outs = refs[3:7]
    coeffs, base, ping, pong, near, whole = refs[7:]
    rows, _, cols = inner.shape
    size = rows + 2 * PAD
    even = place[1] % 2 == 0
    lane = lanes_of((8, LANES))
    half = 2 * STRIP
    own_left, own_right = (STRIP - REACH, cols - (STRIP - REACH))

    def halo(i):
        one = got[0][i]
        two = got[1][i] if pairs_y > 1 else jnp.zeros_like(one)
        return jnp.where(even, two, one), jnp.where(even, one, two)

    def strips(value, left, right):
        first = roll(value[:, :LANES], REACH, 1)
        last = roll(value[:, cols - LANES :], 2 * STRIP - REACH - LANES, 1)
        both = jnp.where(lane < REACH, left, first)
        both = jnp.where(lane < STRIP, both, last)
        return jnp.where(lane < half - REACH, both, right)

    def double(value):
        return jnp.where(lane < half, value, roll(value, half, 1))

    tall = rows + 2 * REACH
    first = pl.cdiv(tall, PER)

    def cell_group(g, _):
        left, right = halo(first + g)

        def field(index, k):
            left_lane = REACH * k + (1 if k == 4 else 0)
            return strips(
                cells_ext[index, g],
                roll(left, -left_lane, 1),
                roll(right, half - REACH - REACH * k, 1),
            )

        viscosity = field(3, 4)
        south_of = jnp.where(lane == 0, roll(left, -4 * REACH, 1), roll(viscosity, 1, 1))
        north_of = jnp.where(
            lane == half - 1,
            roll(right, half - 1 - 4 * REACH - REACH, 1),
            roll(viscosity, -1, 1),
        )
        near[0, g] = double(viscosity)
        near[1, g] = double(south_of)
        near[2, g] = double(north_of)
        near[3, g] = double(field(2, 2))
        near[4, g] = double(field(4, 3))
        near[5, g] = jnp.where(lane < half, field(0, 0), roll(field(1, 1), half, 1))
        return 0

    lax.fori_loop(0, size // 8, cell_group, 0)
    flat = [near[i].reshape(size, LANES) for i in range(6)]
    lane_row = lanes_of((1, LANES))
    along_x = jnp.where(lane_row < half, WEIGHTS[0][0], WEIGHTS[1][0])
    along_y = jnp.where(lane_row < half, WEIGHTS[0][1], WEIGHTS[1][1])
    put_coeffs(coeffs, 0, *flat, along_x, along_y)

    def dir_rows(g, count):
        left, right = halo(g)
        for j in range(count):
            row = PAD - REACH + PER * g + j
            ping[0, row] = double(
                strips(
                    dirs_ext[row],
                    roll(left, -REACH * j, 1),
                    roll(right, half - REACH - REACH * j, 1),
                )
            )

    def dir_group(g, _):
        dir_rows(g, PER)
        return 0

    lax.fori_loop(0, tall // PER, dir_group, 0)
    if tall % PER:
        dir_rows(tall // PER, tall % PER)

    def start(c, j):
        base[0, 8 * c + j] = coeffs[0, 4, c, j : j + 1, :] * ping[0, 8 * c + j]

    def start_chunk(c, _):
        for j in range(8):
            start(c, j)
        return 0

    lax.fori_loop(PAD // 8 - 1, PAD // 8 + rows // 8 + 1, start_chunk, 0)
    for d in range(8, REACH):
        start(PAD // 8 - 2, 15 - d)
        start(PAD // 8 + rows // 8 + 1, d - 8)

    def store(c, j, states):
        value = -(near[5, c, j : j + 1, :] * states[0])
        value = value + roll(value, half, 1)
        row = 8 * c + j - PAD
        old = inner[row]
        whole[row, :, :LANES] = jnp.where(lane < EDGE, roll(value, -REACH, 1), old[:, :LANES])
        whole[row, :, cols - LANES :] = jnp.where(
            lane >= LANES - EDGE,
            roll(value, LANES - half + REACH, 1),
            old[:, cols - LANES :],
        )

    relax(1, coeffs, base, ping, pong, rows, store)
    part = rows // len(outs)
    for k, out in enumerate(outs):
        out[...] = whole[pl.ds(part * (place[2] ^ k), part)]


def gram_of(place, *refs):
    parts, (whole, gram) = refs[:-2], refs[-2:]
    count = len(parts)
    for k, part in enumerate(parts):
        block = pl.multiple_of(8 * (place[2] ^ k), 8)
        for r in range(part.shape[0]):
            whole[r, pl.ds(block, 8), :] = part[r]
    total = jnp.zeros((8 * count, 8 * count), F32)
    for r in range(whole.shape[0]):
        total = total + lax.dot_general(
            whole[r],
            whole[r],
            (((1,), (1,)), ((), ())),
            precision=lax.Precision.HIGHEST,
            preferred_element_type=F32,
        )
    gram[...] = total


def factor(gram, size):
    lane = lanes_of((size, LANES))
    row_of = lax.broadcasted_iota(jnp.int32, (size, LANES), 0)
    wide = jnp.concatenate([gram, jnp.zeros((size, LANES - size), F32)], axis=1)
    work = jnp.where(lane < size, wide, jnp.where(lane == row_of + size, 1.0, 0.0))
    pivots = jnp.ones((size, 1), F32)
    index = lax.broadcasted_iota(jnp.int32, (size, 1), 0)
    for k in range(size):
        top = work[k : k + 1, :]
        pivot = top[:, k : k + 1]
        ratio = jnp.where(index > k, work[:, k : k + 1] / pivot, 0.0)
        pivots = jnp.where(index == k, pivot, pivots)
        work = work - ratio * top
    return work / jnp.sqrt(pivots), lane, row_of


def basis_of(cells, place, gram_ref, whole, *refs):
    outs, upper, scratch = refs[:-2], refs[-2], refs[-1]
    size = gram_ref.shape[0]
    count = len(outs)
    work, lane, row_of = factor(gram_ref[...] / cells, size)
    upper[...] = jnp.where(lane >= row_of, work, 0.0)[:, :size]
    scratch[...] = work
    inverse = jnp.concatenate(
        [
            scratch[pl.ds(pl.multiple_of(8 * (place[2] ^ k), 8), 8), :]
            for k in range(count)
        ],
        axis=0,
    )[:, size : 2 * size]
    for r in range(whole.shape[0]):
        value = jnp.dot(
            inverse, whole[r], precision=lax.Precision.HIGHEST, preferred_element_type=F32
        )
        for k, out in enumerate(outs):
            out[r] = value[8 * k : 8 * k + 8]


def assemble(place, *refs):
    parts, out = refs[:-1], refs[-1]
    for k, part in enumerate(parts):
        rows = part.shape[0]
        base = rows * (place[2] ^ k)
        for c in range(rows // 8):
            out[:, pl.ds(pl.multiple_of(base + 8 * c, 8), 8), :] = jnp.swapaxes(
                part[8 * c : 8 * c + 8], 0, 1
            )


def call(kernel, outs, *args, scratch=(), limit=48):
    smem = pl.BlockSpec(memory_space=pltpu.SMEM)
    vmem = pl.BlockSpec(memory_space=pltpu.VMEM)
    shapes = [jax.ShapeDtypeStruct(shape, F32) for shape in outs]
    return pl.pallas_call(
        kernel,
        out_shape=shapes,
        in_specs=[smem] + [vmem] * (len(args) - 1),
        out_specs=[vmem] * len(shapes),
        scratch_shapes=[pltpu.VMEM(shape, F32) for shape in scratch],
        compiler_params=pltpu.CompilerParams(vmem_limit_bytes=limit << 20),
    )(*args)


def pairings(count):
    sets = []
    for first in (0, 1):
        pairs = [(i, i + 1) for i in range(first, count - 1, 2)]
        if pairs:
            sets.append(pairs + [(j, i) for i, j in pairs])
    return sets


def swap_bit(value, axis, bit):
    count = lax.axis_size(axis)
    return lax.ppermute(value, axis, [(i, i ^ bit) for i in range(count)])


def sum_all(value):
    for axis in ("gy", "gx", "dir"):
        bit = 1
        while bit < lax.axis_size(axis):
            value = value + swap_bit(value, axis, bit)
            bit *= 2
    return value


def on_device(directions, velocity, viscosity, basal_drag, misfit_weight, ice_mask, grounded):
    own, rows, cols = directions.shape
    across = lax.axis_size("dir")
    place = jnp.stack([lax.axis_index(axis) for axis in AXES]).astype(jnp.int32)
    cells = (velocity, viscosity, basal_drag, misfit_weight, ice_mask, grounded)
    groups = rows // 8 + 2 * PAD // 8

    sets_x = pairings(lax.axis_size("gx"))
    row_message = (REACH + 5 * PAD // 8, own, cols)
    messages = call(pack_rows, [row_message] * len(sets_x), place, directions, *cells)
    got_x = [lax.ppermute(m, "gx", s) for m, s in zip(messages, sets_x)]

    sets_y = pairings(lax.axis_size("gy"))
    col_message = (pl.cdiv(rows + 2 * REACH, PER) + groups, own, LANES)
    tall = rows + 2 * PAD
    dirs_ext, cells_ext, *messages = call(
        functools.partial(extend, len(got_x)),
        [(tall, own, cols), (5, groups, 8, cols)] + [col_message] * len(sets_y),
        place,
        *got_x,
        directions,
        *cells,
    )
    got_y = [lax.ppermute(m, "gy", s) for m, s in zip(messages, sets_y)]

    state = (2, tall, own, cols)
    (inner,) = call(
        lambda place, *refs: solve_inner(*refs),
        [(rows, own, cols)],
        place,
        dirs_ext,
        cells_ext,
        scratch=[(2, 6, groups, 8, cols), state, state, state],
    )
    edge_state = (1, tall, own, LANES)
    part = (rows // across, own, cols)
    parts = call(
        functools.partial(solve_edges, len(got_y)),
        [part] * across,
        place,
        *got_y,
        dirs_ext,
        cells_ext,
        inner,
        scratch=[
            (1, 6, groups, 8, LANES),
            edge_state,
            edge_state,
            edge_state,
            (6, groups, 8, LANES),
            (rows, own, cols),
        ],
    )
    parts = [parts[0]] + [swap_bit(parts[k], "dir", k) for k in range(1, across)]
    total = own * across
    whole, gram = call(
        gram_of, [(rows // across, total, cols), (total, total)], place, *parts
    )
    gram = sum_all(gram)
    count = rows * cols * lax.axis_size("gx") * lax.axis_size("gy")
    *parts, upper = call(
        functools.partial(basis_of, float(count)),
        [part] * across + [(total, total)],
        place,
        gram,
        whole,
        scratch=[(total, LANES)],
    )
    parts = [parts[0]] + [swap_bit(parts[k], "dir", k) for k in range(1, across)]
    (basis,) = call(assemble, [(own, rows, cols)], place, *parts)
    return (basis, upper)


def solution(mesh):
    tile = P("gx", "gy")
    placed = (P("dir", "gx", "gy"), P(None, "gx", "gy")) + (tile,) * 5
    return jax.shard_map(
        on_device,
        mesh=mesh,
        in_specs=placed,
        out_specs=(P("dir", "gx", "gy"), P()),
        check_vma=False,
    )
```

```python
import functools

import jax
import jax.numpy as jnp
from jax import lax
from jax.experimental import pallas as pl
from jax.experimental.pallas import tpu as pltpu
from jax.sharding import PartitionSpec as P

SWEEPS = 6
damping = 0.8
KEEP_BACK = 1.0 - damping
REACH = 2 * (SWEEPS - 1)
PAD = 16
LANES = 128
BANDS = 4
SPANS = LANES // BANDS
PLANES = 8
FIELDS = 5
F32 = jnp.float32
BF16 = jnp.bfloat16
AXES = ("gx", "gy", "dir")
WEIGHTS = ((4.0, 1.0), (1.0, 4.0))


def iota(shape, dim):
    return lax.broadcasted_iota(jnp.int32, shape, dim)


def roll(value, shift):
    return pltpu.roll(value, shift % LANES, 1)


def pack(counts, place, *refs):
    count_x, count_y = counts
    sources, refs = refs[:7], refs[7:]
    fields, refs = refs[0], refs[1:]
    row_out, refs = refs[:count_x], refs[count_x:]
    col_out, refs = refs[:count_y], refs[count_y:]
    corner_out, refs = refs[: count_x * count_y], refs[count_x * count_y :]
    held, sems = refs[:7], refs[7]
    copies = [
        pltpu.make_async_copy(source, target, sems.at[i])
        for i, (source, target) in enumerate(zip(sources, held))
    ]
    for copy in copies:
        copy.start()
    for copy in copies[1:]:
        copy.wait()
    dirs, velocity, viscosity, drag, weight, mask, grounded = held
    rows, cols = viscosity.shape
    friction = drag[...] * grounded[...].astype(F32)
    fields[0] = friction * velocity[0]
    fields[1] = friction * velocity[1]
    fields[2] = friction
    fields[3] = viscosity[...]
    fields[4] = weight[...] * mask[...].astype(F32)
    copies[0].wait()

    for pairing, out in enumerate(row_out):
        send_last = place[0] % 2 == pairing
        base = pl.ds(pl.multiple_of(jnp.where(send_last, rows - PAD, 0), PAD), PAD)
        out[:PLANES] = dirs[:, base, :]
        out[PLANES:] = fields[:, base, :]

    lane = iota((8, LANES), 1)
    for g in range(rows // 8):
        span = slice(8 * g, 8 * g + 8)
        for q, (planes, count) in enumerate(((dirs, PLANES), (fields, FIELDS))):
            first = planes[0, span, :LANES]
            last = roll(planes[0, span, cols - LANES :], PAD)
            for p in range(1, count):
                here = lane >= PAD * p
                first = jnp.where(here, roll(planes[p, span, :LANES], PAD * p), first)
                last = jnp.where(
                    here, roll(planes[p, span, cols - LANES :], PAD * (p + 1)), last
                )
            for pairing, out in enumerate(col_out):
                send_last = place[1] % 2 == pairing
                out[q, g] = jnp.where(send_last, last, first)
    for i in range(count_x):
        send_last = place[0] % 2 == i
        base = pl.ds(jnp.where(send_last, (rows - PAD) // 8, 0), PAD // 8)
        for j in range(count_y):
            corner_out[i * count_y + j][...] = col_out[j][:, base]


def exchange_blocks(tiles):
    lane = iota((8, LANES), 1)
    for bit, width in ((1, SPANS), (2, 2 * SPANS)):
        low = (lane // width) % 2 == 0
        tiles = [
            jnp.where(low, tiles[a], roll(tiles[a ^ bit], width))
            if a & bit == 0
            else jnp.where(low, roll(tiles[a ^ bit], -width), tiles[a])
            for a in range(4)
        ]
    return tiles


def split_dot(value, places):
    total = None
    for step in range(3):
        part = value.astype(BF16)
        product = jnp.dot(part, places, preferred_element_type=F32)
        total = product if total is None else total + product
        if step < 2:
            value = value - part.astype(F32)
    return total


def solve(counts, place, *refs):
    count_x, count_y = counts
    got_rows, refs = refs[:count_x], refs[count_x:]
    got_cols, refs = refs[:count_y], refs[count_y:]
    got_corners, refs = refs[: count_x * count_y], refs[count_x * count_y :]
    dirs, fields, *refs = refs
    *outs, halo_rows, halo_cols, lined, turned, planes, coeffs, extras, base, ping, pong = refs
    rows, cols = dirs.shape[1:]
    tall = lined.shape[0]
    over = (tall - rows) // 2
    high = tall // BANDS
    wide = planes.shape[2]
    groups = (rows + 2 * PAD) // 8
    edge = PAD // 8
    even = [place[0] % 2 == 0, place[1] % 2 == 0]

    def sides(axis, one, two):
        return jnp.where(even[axis], two, one), jnp.where(even[axis], one, two)

    def pair(got, index):
        one = got[0][index]
        return one, (got[1][index] if len(got) > 1 else jnp.zeros_like(one))

    for p in range(PLANES + FIELDS):
        halo_rows[0, p], halo_rows[1, p] = sides(0, *pair(got_rows, p))
    for q in range(2):
        left, right = sides(1, *pair(got_cols, q))
        halo_cols[0, q, edge : groups - edge] = left
        halo_cols[1, q, edge : groups - edge] = right
        by_x = [
            sides(1, *pair(got_corners[i * count_y : (i + 1) * count_y], q))
            for i in range(count_x)
        ]
        for side in range(2):
            one = by_x[0][side]
            two = by_x[1][side] if count_x > 1 else jnp.zeros_like(one)
            above, below = sides(0, one, two)
            halo_cols[side, q, :edge] = above
            halo_cols[side, q, groups - edge :] = below

    def spread(shape, source, target):
        k, n = iota(shape, source), iota(shape, target)
        inner = k < cols
        slot = (k - cols) % PAD + jnp.where(k < cols + LANES, 0, cols + PAD)
        at = jnp.where(inner, k + PAD, slot)
        return jnp.where(
            (at == wide * (n % SPANS) + n // SPANS) & (n < wide * SPANS), 1.0, 0.0
        ).astype(BF16)

    lanes_out = turned.shape[2]
    places = spread((cols + 2 * LANES, lanes_out), 0, 1)
    lane = iota((8, LANES), 1)
    own_slot = lane // PAD == iota((8, LANES), 0)

    for q, (source, first, count) in enumerate(((dirs, 0, PLANES), (fields, PLANES, FIELDS))):
        for g in range(groups):
            inner = edge <= g < groups - edge
            side, at = (0, g) if g < edge else (1, g - groups + edge)
            stack = []
            for p in range(PLANES):
                if p >= count:
                    stack.append(jnp.zeros((8, cols), F32))
                elif inner:
                    stack.append(source[p, 8 * (g - edge) : 8 * (g - edge) + 8, :])
                else:
                    stack.append(halo_rows[side, first + p, 8 * at : 8 * at + 8, :])
            lines = jnp.swapaxes(jnp.stack(stack), 0, 1)
            for s in range(8):
                line = 8 * g + s - (PAD - over)
                if 0 <= line < tall:
                    lined[line, :, :cols] = lines[s]
                    for side_y in range(2):
                        begin = cols + LANES * side_y
                        lined[line, :, begin : begin + LANES] = jnp.where(
                            own_slot, halo_cols[side_y, q, g, s : s + 1, :], 0.0
                        )

        def turn(b, _):
            value = lined[pl.ds(high * b, high)].reshape(high * 8, cols + 2 * LANES)
            turned[pl.ds(high * b, high)] = split_dot(value, places).reshape(
                high, 8, lanes_out
            )
            return 0

        lax.fori_loop(0, BANDS, turn, 0)

        def band(i, _):
            for t in range(lanes_out // LANES):
                tiles = [
                    turned[high * b + i, :, LANES * t : LANES * t + LANES] for b in range(BANDS)
                ]
                tiles = exchange_blocks(tiles)
                for a in range(BANDS):
                    if BANDS * t + a < wide:
                        planes[q, i, BANDS * t + a] = tiles[a]
            return 0

        lax.fori_loop(0, high, band, 0)

    row_of = iota((8, LANES), 0)

    def weigh(i, above, below, turn_above, turn_below):
        def field(k, row, j):
            return jnp.broadcast_to(planes[1, row, j, k : k + 1, :], (8, LANES))

        mids = [field(3, i, j) for j in range(wide)]
        wests = [roll(mids[-1], 1)] + mids[:-1]
        easts = mids[1:] + [roll(mids[0], -1)]
        for j in range(wide):
            mid = mids[j]
            up, down = field(3, above, j), field(3, below, j)
            up = roll(up, SPANS) if turn_above else up
            down = roll(down, -SPANS) if turn_below else down
            east, west = 0.5 * (mid + down), 0.5 * (mid + up)
            north, south = 0.5 * (mid + easts[j]), 0.5 * (mid + wests[j])
            along_x, along_y = east + west, north + south
            friction, kept = field(2, i, j), field(4, i, j)

            def step(is_first):
                ax = jnp.where(is_first, WEIGHTS[0][0], WEIGHTS[1][0])
                ay = jnp.where(is_first, WEIGHTS[0][1], WEIGHTS[1][1])
                diagonal = ax * along_x + ay * along_y + friction
                return ax, ay, jnp.where(kept != 0.0, damping / diagonal, 0.0)

            ax, ay, gain = step(row_of < 4)
            kind = row_of % 4
            face = jnp.where(kind < 2, jnp.where(kind == 0, east, west), jnp.where(kind == 2, north, south))
            coeffs[i, j] = gain * jnp.where(kind < 2, ax, ay) * face
            _, _, gain = step(row_of % 2 == 0)
            pull = -jnp.where(row_of % 2 == 0, field(0, i, j), field(1, i, j))
            extras[i, j] = jnp.where(
                row_of < 4, gain * jnp.where(row_of < 2, pull, kept), pull
            )

    weigh(0, high - 1, 1, True, False)
    weigh(high - 1, high - 2, 0, False, True)

    def weigh_inner(i, _):
        weigh(i, i - 1, i + 1, False, False)
        return 0

    lax.fori_loop(1, high - 1, weigh_inner, 0)

    def put(ref, m, i, j, value, edges=True):
        ref[m, i + 1, j] = value
        if edges and isinstance(i, int):
            if i == 0:
                ref[m, high + 1, j] = roll(value, -SPANS)
            if i == high - 1:
                ref[m, 0, j] = roll(value, SPANS)

    def over_rows(body):
        body(0)
        body(high - 1)

        def two(i, _):
            body(2 * i + 1)
            body(2 * i + 2)
            return 0

        lax.fori_loop(0, (high - 2) // 2, two, 0)

    def start(i):
        for j in range(wide):
            for m in range(2):
                put(base, m, i, j, extras[i, j, m : m + 1, :] * planes[0, i, j])

    over_rows(start)

    def sweep(source, store):
        def body(i):
            for m in range(2):
                mids = [source[m, i + 1, j] for j in range(wide)]
                before = [roll(mids[-1], 1)] + mids[:-1]
                after = mids[1:] + [roll(mids[0], -1)]
                for j in range(wide):
                    e, w, n, s = (coeffs[i, j, 4 * m + d : 4 * m + d + 1, :] for d in range(4))
                    store(
                        m,
                        i,
                        j,
                        (base[m, i + 1, j] + KEEP_BACK * mids[j])
                        + (e * source[m, i + 2, j] + w * source[m, i, j])
                        + (n * after[j] + s * before[j]),
                    )

        over_rows(body)

    def to(ref):
        return lambda m, i, j, value: put(ref, m, i, j, value)

    def to_adjoint(m, i, j, value):
        pong[m, i + 1, j] = extras[i, j, 2 + m : 3 + m, :] * value

    def to_sketch(m, i, j, value):
        value = extras[i, j, 4 + m : 5 + m, :] * value
        planes[0, i, j] = value if m == 0 else planes[0, i, j] + value

    for part in range(2):
        source = base
        for step in range(SWEEPS - 2):
            target = ping if source is not ping else pong
            sweep(source, to(target))
            source = target
        if part == 0:
            target = ping if source is not ping else pong

            def adjoint(m, i, j, value, target=target):
                put(target, m, i, j, extras[i, j, 2 + m : 3 + m, :] * value)

            sweep(source, adjoint)
            base, ping, pong = target, base, source
        else:
            sweep(source, to_sketch)

    def unband(i, _):
        for t in range(lanes_out // LANES):
            tiles = [
                planes[0, i, BANDS * t + a] if BANDS * t + a < wide else jnp.zeros((8, LANES), F32)
                for a in range(BANDS)
            ]
            tiles = exchange_blocks(tiles)
            for b in range(BANDS):
                turned[high * b + i, :, LANES * t : LANES * t + LANES] = tiles[b]
        return 0

    lax.fori_loop(0, high, unband, 0)
    places = spread((lanes_out, cols), 1, 0)
    part = rows // len(outs)
    for k, out in enumerate(outs):
        value = turned[pl.ds(over + part * (place[2] ^ k), part)].reshape(part * 8, lanes_out)
        out[...] = split_dot(value, places).reshape(part, 8, cols)


def gram_of(place, *refs):
    parts, (whole, gram) = refs[:-2], refs[-2:]
    count = len(parts)
    for k, part in enumerate(parts):
        block = pl.multiple_of(8 * (place[2] ^ k), 8)
        for r in range(part.shape[0]):
            whole[r, pl.ds(block, 8), :] = part[r]
    total = jnp.zeros((8 * count, 8 * count), F32)
    for r in range(whole.shape[0]):
        total = total + lax.dot_general(
            whole[r],
            whole[r],
            (((1,), (1,)), ((), ())),
            precision=lax.Precision.HIGHEST,
            preferred_element_type=F32,
        )
    gram[...] = total


def factor(gram, size):
    lane = iota((size, LANES), 1)
    row_of = iota((size, LANES), 0)
    wide = jnp.concatenate([gram, jnp.zeros((size, LANES - size), F32)], axis=1)
    work = jnp.where(lane < size, wide, jnp.where(lane == row_of + size, 1.0, 0.0))
    pivots = jnp.ones((size, 1), F32)
    index = iota((size, 1), 0)
    for k in range(size):
        top = work[k : k + 1, :]
        pivot = top[:, k : k + 1]
        ratio = jnp.where(index > k, work[:, k : k + 1] / pivot, 0.0)
        pivots = jnp.where(index == k, pivot, pivots)
        work = work - ratio * top
    return work / jnp.sqrt(pivots), lane, row_of


def basis_of(cells, place, gram_ref, whole, *refs):
    outs, upper, scratch = refs[:-2], refs[-2], refs[-1]
    size = gram_ref.shape[0]
    count = len(outs)
    work, lane, row_of = factor(gram_ref[...] / cells, size)
    upper[...] = jnp.where(lane >= row_of, work, 0.0)[:, :size]
    scratch[...] = work
    inverse = jnp.concatenate(
        [
            scratch[pl.ds(pl.multiple_of(8 * (place[2] ^ k), 8), 8), :]
            for k in range(count)
        ],
        axis=0,
    )[:, size : 2 * size]
    for r in range(whole.shape[0]):
        value = jnp.dot(
            inverse, whole[r], precision=lax.Precision.HIGHEST, preferred_element_type=F32
        )
        for k, out in enumerate(outs):
            out[r] = value[8 * k : 8 * k + 8]


def assemble(place, *refs):
    parts, out = refs[:-1], refs[-1]
    for k, part in enumerate(parts):
        rows = part.shape[0]
        base = rows * (place[2] ^ k)
        for c in range(rows // 8):
            out[:, pl.ds(pl.multiple_of(base + 8 * c, 8), 8), :] = jnp.swapaxes(
                part[8 * c : 8 * c + 8], 0, 1
            )


def call(kernel, outs, *args, scratch=(), limit=56, space=pltpu.VMEM):
    smem = pl.BlockSpec(memory_space=pltpu.SMEM)
    vmem = pl.BlockSpec(memory_space=pltpu.VMEM)
    shapes = [jax.ShapeDtypeStruct(shape, F32) for shape in outs]
    return pl.pallas_call(
        kernel,
        out_shape=shapes,
        in_specs=[smem] + [pl.BlockSpec(memory_space=space)] * (len(args) - 1),
        out_specs=[vmem] * len(shapes),
        scratch_shapes=[
            pltpu.VMEM(shape, F32) if isinstance(shape, tuple) else shape for shape in scratch
        ],
        compiler_params=pltpu.CompilerParams(vmem_limit_bytes=limit << 20),
    )(*args)


def pairings(count):
    sets = []
    for first in (0, 1):
        pairs = [(i, i + 1) for i in range(first, count - 1, 2)]
        if pairs:
            sets.append(pairs + [(j, i) for i, j in pairs])
    return sets


def swap_bit(value, axis, bit):
    count = lax.axis_size(axis)
    return lax.ppermute(value, axis, [(i, i ^ bit) for i in range(count)])


def sum_all(value):
    for axis in ("gy", "gx", "dir"):
        bit = 1
        while bit < lax.axis_size(axis):
            value = value + swap_bit(value, axis, bit)
            bit *= 2
    return value


def on_device(directions, velocity, viscosity, basal_drag, misfit_weight, ice_mask, grounded):
    own, rows, cols = directions.shape
    across = lax.axis_size("dir")
    place = jnp.stack([lax.axis_index(axis) for axis in AXES]).astype(jnp.int32)
    args = (directions, velocity, viscosity, basal_drag, misfit_weight, ice_mask, grounded)

    count_y = lax.axis_size("gy")
    sets_x, sets_y = pairings(lax.axis_size("gx")), pairings(count_y)
    counts = (len(sets_x), len(sets_y))
    fields, *messages = call(
        functools.partial(pack, counts),
        [(FIELDS, rows, cols)]
        + [(PLANES + FIELDS, PAD, cols)] * counts[0]
        + [(2, rows // 8, 8, LANES)] * counts[1]
        + [(2, PAD // 8, 8, LANES)] * (counts[0] * counts[1]),
        place,
        *args,
        scratch=[pltpu.VMEM(a.shape, a.dtype) for a in args] + [pltpu.SemaphoreType.DMA((7,))],
        space=pl.ANY,
    )
    moves = [("gx", s) for s in sets_x] + [("gy", s) for s in sets_y]
    for set_x in sets_x:
        for set_y in sets_y:
            pairs = [(a * count_y + c, b * count_y + d) for a, b in set_x for c, d in set_y]
            moves.append((("gx", "gy"), pairs))
    got = [lax.ppermute(m, axis, pairs) for m, (axis, pairs) in zip(messages, moves)]

    over = REACH + 2
    tall = rows + 2 * over
    wide = pl.cdiv(cols + 2 * PAD, SPANS)
    groups = (rows + 2 * PAD) // 8
    high = tall // BANDS
    lanes_out = pl.cdiv(wide, BANDS) * LANES
    state = (2, high + 2, wide, 8, LANES)
    part = (rows // across, own, cols)
    parts = call(
        functools.partial(solve, counts),
        [part] * across,
        place,
        *got,
        directions,
        fields,
        scratch=[
            (2, PLANES + FIELDS, PAD, cols),
            (2, 2, groups, 8, LANES),
            (tall, 8, cols + 2 * LANES),
            (tall, 8, lanes_out),
            (2, high, wide, 8, LANES),
            (high, wide, 8, LANES),
            (high, wide, 8, LANES),
            state,
            state,
            state,
        ],
    )
    parts = [parts[0]] + [swap_bit(parts[k], "dir", k) for k in range(1, across)]
    total = own * across
    whole, gram = call(
        gram_of, [(rows // across, total, cols), (total, total)], place, *parts
    )
    gram = sum_all(gram)
    count = rows * cols * lax.axis_size("gx") * lax.axis_size("gy")
    *parts, upper = call(
        functools.partial(basis_of, float(count)),
        [part] * across + [(total, total)],
        place,
        gram,
        whole,
        scratch=[(total, LANES)],
    )
    parts = [parts[0]] + [swap_bit(parts[k], "dir", k) for k in range(1, across)]
    (basis,) = call(assemble, [(own, rows, cols)], place, *parts)
    return (basis, upper)


def solution(mesh):
    tile = P("gx", "gy")
    placed = (P("dir", "gx", "gy"), P(None, "gx", "gy")) + (tile,) * 5
    return jax.shard_map(
        on_device,
        mesh=mesh,
        in_specs=placed,
        out_specs=(P("dir", "gx", "gy"), P()),
        check_vma=False,
    )
```

```python
import functools

import jax
import jax.numpy as jnp
import numpy as np
from jax import lax
from jax.experimental import pallas as pl
from jax.experimental.pallas import tpu as pltpu
from jax.sharding import PartitionSpec as P

SWEEPS = 6
damping = 0.8
KEEP_BACK = 1.0 - damping
GROWN, SHRUNK = 1.0 + KEEP_BACK, 1.0 - KEEP_BACK
REACH = 2 * (SWEEPS - 1)
PAD = 16
LANES = 128
BANDS = 4
SPANS = LANES // BANDS
PLANES = 8
FIELDS = 5
F32 = jnp.float32
BF16 = jnp.bfloat16
AXES = ("gx", "gy", "dir")
WEIGHTS = ((4.0, 1.0), (1.0, 4.0))
PARTS = 2
UNROLL = 3


def iota(shape, dim):
    return lax.broadcasted_iota(jnp.int32, shape, dim)


def roll(value, shift):
    return pltpu.roll(value, shift % LANES, 1)


def pack(counts, place, *refs):
    count_x, count_y = counts
    sources, refs = refs[:7], refs[7:]
    fields, refs = refs[0], refs[1:]
    row_out, refs = refs[:count_x], refs[count_x:]
    col_out, refs = refs[:count_y], refs[count_y:]
    corner_out, refs = refs[: count_x * count_y], refs[count_x * count_y :]
    held, sems = refs[:7], refs[7]
    copies = [
        pltpu.make_async_copy(source, target, sems.at[i])
        for i, (source, target) in enumerate(zip(sources, held))
    ]
    for copy in copies:
        copy.start()
    for copy in copies[1:]:
        copy.wait()
    dirs, velocity, viscosity, drag, weight, mask, grounded = held
    rows, cols = viscosity.shape
    friction = drag[...] * grounded[...].astype(F32)
    fields[0] = friction * velocity[0]
    fields[1] = friction * velocity[1]
    fields[2] = friction
    fields[3] = viscosity[...]
    fields[4] = weight[...] * mask[...].astype(F32)
    copies[0].wait()

    for pairing, out in enumerate(row_out):
        send_last = place[0] % 2 == pairing
        base = pl.ds(pl.multiple_of(jnp.where(send_last, rows - PAD, 0), PAD), PAD)
        out[:PLANES] = dirs[:, base, :]
        out[PLANES:] = fields[:, base, :]

    lane = iota((8, LANES), 1)
    for g in range(rows // 8):
        span = slice(8 * g, 8 * g + 8)
        for q, (planes, count) in enumerate(((dirs, PLANES), (fields, FIELDS))):
            first = planes[0, span, :LANES]
            last = roll(planes[0, span, cols - LANES :], PAD)
            for p in range(1, count):
                here = lane >= PAD * p
                first = jnp.where(here, roll(planes[p, span, :LANES], PAD * p), first)
                last = jnp.where(
                    here, roll(planes[p, span, cols - LANES :], PAD * (p + 1)), last
                )
            for pairing, out in enumerate(col_out):
                send_last = place[1] % 2 == pairing
                out[q, g] = jnp.where(send_last, last, first)
    for i in range(count_x):
        send_last = place[0] % 2 == i
        base = pl.ds(jnp.where(send_last, (rows - PAD) // 8, 0), PAD // 8)
        for j in range(count_y):
            corner_out[i * count_y + j][...] = col_out[j][:, base]


def from_bands(tiles):
    block = iota((8, LANES), 1) // SPANS
    out = []
    for column in range(BANDS):
        value = tiles[0]
        for band in range(1, BANDS):
            value = jnp.where(block == (column + band) % BANDS, tiles[band], value)
        out.append(roll(value, -SPANS * column) if column else value)
    return out


def to_bands(tiles):
    block = iota((8, LANES), 1) // SPANS
    turned = [roll(tile, SPANS * column) if column else tile for column, tile in enumerate(tiles)]
    out = []
    for band in range(BANDS):
        value = turned[0]
        for column in range(1, BANDS):
            value = jnp.where(block == (column + band) % BANDS, turned[column], value)
        out.append(value)
    return out


def band_places(cols, wide):
    slot = np.arange(LANES) % PAD
    column = np.concatenate([np.arange(cols) + PAD, slot, slot + cols + PAD])
    span, j = column // wide, column % wide
    out = np.zeros((BANDS, column.size, pl.cdiv(wide, BANDS) * LANES), np.float32)
    for band in range(BANDS):
        lane = LANES * (j // BANDS) + SPANS * ((j + band) % BANDS) + span
        out[band, np.arange(column.size), lane] = 1.0
    return out.astype(BF16)


def split_dot(value, places, transposed=False):
    total = None
    for step in range(PARTS):
        part = value.astype(BF16)
        product = lax.dot_general(
            part,
            places,
            (((1,), (1 if transposed else 0,)), ((), ())),
            preferred_element_type=F32,
        )
        total = product if total is None else total + product
        if step < PARTS - 1:
            value = value - part.astype(F32)
    return total


def solve(counts, place, *refs):
    count_x, count_y = counts
    got_rows, refs = refs[:count_x], refs[count_x:]
    got_cols, refs = refs[:count_y], refs[count_y:]
    got_corners, refs = refs[: count_x * count_y], refs[count_x * count_y :]
    dirs, fields, places, *refs = refs
    *outs, halo_rows, halo_cols, lined, turned, planes, coeffs, extras, base, ping, pong = refs
    rows, cols = dirs.shape[1:]
    tall = lined.shape[0]
    over = (tall - rows) // 2
    high = tall // BANDS
    wide = planes.shape[2]
    groups = (rows + 2 * PAD) // 8
    edge = PAD // 8
    even = [place[0] % 2 == 0, place[1] % 2 == 0]

    def sides(axis, one, two):
        return jnp.where(even[axis], two, one), jnp.where(even[axis], one, two)

    def pair(got, index):
        one = got[0][index]
        return one, (got[1][index] if len(got) > 1 else jnp.zeros_like(one))

    for p in range(PLANES + FIELDS):
        halo_rows[0, p], halo_rows[1, p] = sides(0, *pair(got_rows, p))
    for q in range(2):
        left, right = sides(1, *pair(got_cols, q))
        halo_cols[0, q, edge : groups - edge] = left
        halo_cols[1, q, edge : groups - edge] = right
        by_x = [
            sides(1, *pair(got_corners[i * count_y : (i + 1) * count_y], q))
            for i in range(count_x)
        ]
        for side in range(2):
            one = by_x[0][side]
            two = by_x[1][side] if count_x > 1 else jnp.zeros_like(one)
            above, below = sides(0, one, two)
            halo_cols[side, q, :edge] = above
            halo_cols[side, q, groups - edge :] = below

    lanes_out = turned.shape[2]
    lane = iota((8, LANES), 1)
    own_slot = lane // PAD == iota((8, LANES), 0)

    def over_pairs(body):
        def two(i, _):
            body(2 * i)
            body(2 * i + 1)
            return 0

        lax.fori_loop(0, high // 2, two, 0)

    for q, (source, first, count) in enumerate(((dirs, 0, PLANES), (fields, PLANES, FIELDS))):
        for g in range(groups):
            inner = edge <= g < groups - edge
            side, at = (0, g) if g < edge else (1, g - groups + edge)
            stack = []
            for p in range(PLANES):
                if p >= count:
                    stack.append(jnp.zeros((8, cols), F32))
                elif inner:
                    stack.append(source[p, 8 * (g - edge) : 8 * (g - edge) + 8, :])
                else:
                    stack.append(halo_rows[side, first + p, 8 * at : 8 * at + 8, :])
            lines = jnp.swapaxes(jnp.stack(stack), 0, 1)
            for s in range(8):
                line = 8 * g + s - (PAD - over)
                if 0 <= line < tall:
                    lined[line, :, :cols] = lines[s]
                    for side_y in range(2):
                        begin = cols + LANES * side_y
                        lined[line, :, begin : begin + LANES] = jnp.where(
                            own_slot, halo_cols[side_y, q, g, s : s + 1, :], 0.0
                        )

        def turn(b, _):
            value = lined[pl.ds(high * b, high)].reshape(high * 8, cols + 2 * LANES)
            turned[pl.ds(high * b, high)] = split_dot(value, places[b]).reshape(
                high, 8, lanes_out
            )
            return 0

        lax.fori_loop(0, BANDS, turn, 0)

        def band(i):
            for t in range(lanes_out // LANES):
                tiles = [
                    turned[high * b + i, :, LANES * t : LANES * t + LANES] for b in range(BANDS)
                ]
                for j, tile in enumerate(from_bands(tiles)[: wide - BANDS * t], BANDS * t):
                    planes[q, i, j] = tile

        over_pairs(band)

    row_of = iota((8, LANES), 0)
    kind = row_of % 4
    ax = jnp.where(row_of < 4, WEIGHTS[0][0], WEIGHTS[1][0])
    ay = jnp.where(row_of < 4, WEIGHTS[0][1], WEIGHTS[1][1])
    along = jnp.where(kind < 2, ax, ay)

    def weigh(i, above, below, turn_above, turn_below):
        def field(k, row, j):
            return jnp.broadcast_to(planes[1, row, j, k : k + 1, :], (8, LANES))

        mids = [field(3, i, j) for j in range(wide)]
        wests = [roll(mids[-1], 1)] + mids[:-1]
        easts = mids[1:] + [roll(mids[0], -1)]
        for j in range(wide):
            mid = mids[j]
            up, down = field(3, above, j), field(3, below, j)
            up = roll(up, SPANS) if turn_above else up
            down = roll(down, -SPANS) if turn_below else down
            east, west = 0.5 * (mid + down), 0.5 * (mid + up)
            north, south = 0.5 * (mid + easts[j]), 0.5 * (mid + wests[j])
            along_x, along_y = east + west, north + south
            friction, kept = field(2, i, j), field(4, i, j)

            diagonal = ax * along_x + ay * along_y + friction
            gain = jnp.where(kept != 0.0, damping / diagonal, 0.0)
            face = jnp.where(
                kind < 2,
                jnp.where(kind == 0, east, west),
                jnp.where(kind == 2, north, south),
            )
            weight = gain * along * face
            coeffs[0, i, j] = weight * (1.0 / GROWN)
            coeffs[1, i, j] = weight * (1.0 / KEEP_BACK)
            coeffs[2, i, j] = weight * (-1.0 / SHRUNK)
            pull = jnp.where(row_of < 4, field(0, i, j), field(1, i, j))
            extras[i, j] = jnp.where(
                kind == 1,
                GROWN * gain * kept,
                jnp.where(kind == 0, gain, GROWN) * -pull,
            )

    weigh(0, high - 1, 1, True, False)
    weigh(high - 1, high - 2, 0, False, True)

    def weigh_inner(i, _):
        weigh(i, i - 1, i + 1, False, False)
        return 0

    lax.fori_loop(1, high - 1, weigh_inner, 0)

    def put(ref, m, i, j, value, edges=True):
        ref[m, i + 1, j] = value
        if edges and isinstance(i, int):
            if i == 0:
                ref[m, high + 1, j] = roll(value, -SPANS)
            if i == high - 1:
                ref[m, 0, j] = roll(value, SPANS)

    def over_rows(body):
        body(0)
        body(high - 1)

        def some(i, _):
            for d in range(UNROLL):
                body(UNROLL * i + d + 1)
            return 0

        full = (high - 2) // UNROLL
        lax.fori_loop(0, full, some, 0)
        for i in range(1 + UNROLL * full, high - 1):
            body(i)

    def extra(kind, m, i, j):
        return extras[i, j, 4 * m + kind : 4 * m + kind + 1, :]

    def start(i):
        for j in range(wide):
            for m in range(2):
                put(base, m, i, j, extra(0, m, i, j) * planes[0, i, j])

    over_rows(start)

    def sweep(source, scale, store):
        def body(i):
            for m in range(2):
                mids = [source[m, i + 1, j] for j in range(wide)]
                before = [roll(mids[-1], 1)] + mids[:-1]
                after = mids[1:] + [roll(mids[0], -1)]
                for j in range(wide):
                    e, w, n, s = (
                        coeffs[scale, i, j, 4 * m + d : 4 * m + d + 1, :] for d in range(4)
                    )
                    along_x = e * source[m, i + 2, j] + w * source[m, i, j]
                    along_y = n * after[j] + s * before[j]
                    store(m, i, j, mids[j] + (along_x + along_y))

        over_rows(body)

    def to(ref):
        return lambda m, i, j, value: put(ref, m, i, j, value)

    def solve_from(one, two, three, store):
        sweep(one, 0, to(two))
        sweep(two, 1, to(three))

        def add(m, i, j, value):
            put(one, m, i, j, two[m, i + 1, j] + (KEEP_BACK * GROWN) * value)

        sweep(three, 0, add)
        sweep(one, 1, to(three))

        def last(m, i, j, value):
            store(m, i, j, one[m, i + 1, j] - (KEEP_BACK * SHRUNK) * value)

        sweep(three, 2, last)

    def to_adjoint(m, i, j, value):
        put(ping, m, i, j, extra(1, m, i, j) * value)

    def to_sketch(m, i, j, value):
        value = extra(2, m, i, j) * value
        planes[0, i, j] = value if m == 0 else planes[0, i, j] + value

    solve_from(base, ping, pong, to_adjoint)
    solve_from(ping, base, pong, to_sketch)

    def unband(i):
        for t in range(lanes_out // LANES):
            tiles = [planes[0, i, j] for j in range(BANDS * t, min(BANDS * t + BANDS, wide))]
            tiles += [jnp.zeros((8, LANES), F32)] * (BANDS - len(tiles))
            for b, tile in enumerate(to_bands(tiles)):
                turned[high * b + i, :, LANES * t : LANES * t + LANES] = tile

    over_pairs(unband)

    def unturn(b, _):
        value = turned[pl.ds(high * b, high)].reshape(high * 8, lanes_out)
        value = split_dot(value, places[b, :cols, :], transposed=True)
        lined[pl.ds(high * b, high), :, :cols] = value.reshape(high, 8, cols)
        return 0

    lax.fori_loop(0, BANDS, unturn, 0)
    part = rows // len(outs)
    for k, out in enumerate(outs):
        out[...] = lined[pl.ds(over + part * (place[2] ^ k), part), :, :cols]


def gram_of(place, *refs):
    parts, (whole, gram) = refs[:-2], refs[-2:]
    count = len(parts)
    for k, part in enumerate(parts):
        block = pl.multiple_of(8 * (place[2] ^ k), 8)
        for r in range(part.shape[0]):
            whole[r, pl.ds(block, 8), :] = part[r]
    total = jnp.zeros((8 * count, 8 * count), F32)
    for r in range(whole.shape[0]):
        total = total + lax.dot_general(
            whole[r],
            whole[r],
            (((1,), (1,)), ((), ())),
            precision=lax.Precision.HIGHEST,
            preferred_element_type=F32,
        )
    gram[...] = total


def factor(gram, size):
    lane = iota((size, LANES), 1)
    row_of = iota((size, LANES), 0)
    wide = jnp.concatenate([gram, jnp.zeros((size, LANES - size), F32)], axis=1)
    work = jnp.where(lane < size, wide, jnp.where(lane == row_of + size, 1.0, 0.0))
    pivots = jnp.ones((size, 1), F32)
    index = iota((size, 1), 0)
    for k in range(size):
        top = work[k : k + 1, :]
        pivot = top[:, k : k + 1]
        ratio = jnp.where(index > k, work[:, k : k + 1] / pivot, 0.0)
        pivots = jnp.where(index == k, pivot, pivots)
        work = work - ratio * top
    return work / jnp.sqrt(pivots), lane, row_of


def basis_of(cells, place, gram_ref, whole, *refs):
    outs, upper, scratch = refs[:-2], refs[-2], refs[-1]
    size = gram_ref.shape[0]
    count = len(outs)
    work, lane, row_of = factor(gram_ref[...] / cells, size)
    upper[...] = jnp.where(lane >= row_of, work, 0.0)[:, :size]
    scratch[...] = work
    inverse = jnp.concatenate(
        [
            scratch[pl.ds(pl.multiple_of(8 * (place[2] ^ k), 8), 8), :]
            for k in range(count)
        ],
        axis=0,
    )[:, size : 2 * size]
    for r in range(whole.shape[0]):
        value = jnp.dot(
            inverse, whole[r], precision=lax.Precision.HIGHEST, preferred_element_type=F32
        )
        for k, out in enumerate(outs):
            out[r] = value[8 * k : 8 * k + 8]


def assemble(place, *refs):
    parts, out = refs[:-1], refs[-1]
    for k, part in enumerate(parts):
        rows = part.shape[0]
        base = rows * (place[2] ^ k)
        for c in range(rows // 8):
            out[:, pl.ds(pl.multiple_of(base + 8 * c, 8), 8), :] = jnp.swapaxes(
                part[8 * c : 8 * c + 8], 0, 1
            )


def call(kernel, outs, *args, scratch=(), limit=56, space=pltpu.VMEM):
    smem = pl.BlockSpec(memory_space=pltpu.SMEM)
    vmem = pl.BlockSpec(memory_space=pltpu.VMEM)
    shapes = [jax.ShapeDtypeStruct(shape, F32) for shape in outs]
    return pl.pallas_call(
        kernel,
        out_shape=shapes,
        in_specs=[smem] + [pl.BlockSpec(memory_space=space)] * (len(args) - 1),
        out_specs=[vmem] * len(shapes),
        scratch_shapes=[
            pltpu.VMEM(shape, F32) if isinstance(shape, tuple) else shape for shape in scratch
        ],
        compiler_params=pltpu.CompilerParams(vmem_limit_bytes=limit << 20),
    )(*args)


def pairings(count):
    sets = []
    for first in (0, 1):
        pairs = [(i, i + 1) for i in range(first, count - 1, 2)]
        if pairs:
            sets.append(pairs + [(j, i) for i, j in pairs])
    return sets


def swap_bit(value, axis, bit):
    count = lax.axis_size(axis)
    return lax.ppermute(value, axis, [(i, i ^ bit) for i in range(count)])


def sum_all(value):
    for axis in ("gy", "gx", "dir"):
        bit = 1
        while bit < lax.axis_size(axis):
            value = value + swap_bit(value, axis, bit)
            bit *= 2
    return value


def on_device(directions, velocity, viscosity, basal_drag, misfit_weight, ice_mask, grounded):
    own, rows, cols = directions.shape
    across = lax.axis_size("dir")
    place = jnp.stack([lax.axis_index(axis) for axis in AXES]).astype(jnp.int32)
    args = (directions, velocity, viscosity, basal_drag, misfit_weight, ice_mask, grounded)

    count_y = lax.axis_size("gy")
    sets_x, sets_y = pairings(lax.axis_size("gx")), pairings(count_y)
    counts = (len(sets_x), len(sets_y))
    fields, *messages = call(
        functools.partial(pack, counts),
        [(FIELDS, rows, cols)]
        + [(PLANES + FIELDS, PAD, cols)] * counts[0]
        + [(2, rows // 8, 8, LANES)] * counts[1]
        + [(2, PAD // 8, 8, LANES)] * (counts[0] * counts[1]),
        place,
        *args,
        scratch=[pltpu.VMEM(a.shape, a.dtype) for a in args] + [pltpu.SemaphoreType.DMA((7,))],
        space=pl.ANY,
    )
    moves = [("gx", s) for s in sets_x] + [("gy", s) for s in sets_y]
    for set_x in sets_x:
        for set_y in sets_y:
            pairs = [(a * count_y + c, b * count_y + d) for a, b in set_x for c, d in set_y]
            moves.append((("gx", "gy"), pairs))
    got = [lax.ppermute(m, axis, pairs) for m, (axis, pairs) in zip(messages, moves)]

    over = REACH + 2
    tall = rows + 2 * over
    wide = pl.cdiv(cols + 2 * PAD, SPANS)
    groups = (rows + 2 * PAD) // 8
    high = tall // BANDS
    lanes_out = pl.cdiv(wide, BANDS) * LANES
    state = (2, high + 2, wide, 8, LANES)
    part = (rows // across, own, cols)
    parts = call(
        functools.partial(solve, counts),
        [part] * across,
        place,
        *got,
        directions,
        fields,
        band_places(cols, wide),
        scratch=[
            (2, PLANES + FIELDS, PAD, cols),
            (2, 2, groups, 8, LANES),
            (tall, 8, cols + 2 * LANES),
            (tall, 8, lanes_out),
            (2, high, wide, 8, LANES),
            (3, high, wide, 8, LANES),
            (high, wide, 8, LANES),
            state,
            state,
            state,
        ],
    )
    parts = [parts[0]] + [swap_bit(parts[k], "dir", k) for k in range(1, across)]
    total = own * across
    whole, gram = call(
        gram_of, [(rows // across, total, cols), (total, total)], place, *parts
    )
    gram = sum_all(gram)
    count = rows * cols * lax.axis_size("gx") * lax.axis_size("gy")
    *parts, upper = call(
        functools.partial(basis_of, float(count)),
        [part] * across + [(total, total)],
        place,
        gram,
        whole,
        scratch=[(total, LANES)],
    )
    parts = [parts[0]] + [swap_bit(parts[k], "dir", k) for k in range(1, across)]
    (basis,) = call(assemble, [(own, rows, cols)], place, *parts)
    return (basis, upper)


def solution(mesh):
    tile = P("gx", "gy")
    placed = (P("dir", "gx", "gy"), P(None, "gx", "gy")) + (tile,) * 5
    return jax.shard_map(
        on_device,
        mesh=mesh,
        in_specs=placed,
        out_specs=(P("dir", "gx", "gy"), P()),
        check_vma=False,
    )
```

```python
import functools

import jax
import jax.numpy as jnp
import numpy as np
from jax import lax
from jax.experimental import pallas as pl
from jax.experimental.pallas import tpu as pltpu
from jax.sharding import PartitionSpec as P

SWEEPS = 6
damping = 0.8
KEEP_BACK = 1.0 - damping
GROWN, SHRUNK = 1.0 + KEEP_BACK, 1.0 - KEEP_BACK
REACH = 2 * (SWEEPS - 1)
PAD = 16
LANES = 128
BANDS = 4
SPANS = LANES // BANDS
PLANES = 8
FIELDS = 5
F32 = jnp.float32
BF16 = jnp.bfloat16
WEIGHTS = ((4.0, 1.0), (1.0, 4.0))
PARTS = 2
FIRST_ROWS = 80


def iota(shape, dim):
    return lax.broadcasted_iota(jnp.int32, shape, dim)


def roll(value, shift):
    return pltpu.roll(value, shift % LANES, 1)


def pack(counts, *refs):
    count_x, count_y = counts
    sources, refs = refs[:7], refs[7:]
    fields, refs = refs[0], refs[1:]
    row_out, refs = refs[:count_x], refs[count_x:]
    col_out, refs = refs[:count_y], refs[count_y:]
    corner_out, refs = refs[: count_x * count_y], refs[count_x * count_y :]
    held, sems = refs[:7], refs[7]
    copies = [
        pltpu.make_async_copy(source, target, sems.at[i])
        for i, (source, target) in enumerate(zip(sources, held))
    ]
    for copy in copies:
        copy.start()
    for copy in copies[1:]:
        copy.wait()
    dirs, velocity, viscosity, drag, weight, mask, grounded = held
    rows, cols = viscosity.shape
    friction = drag[...] * grounded[...].astype(F32)
    fields[0] = friction * velocity[0]
    fields[1] = friction * velocity[1]
    fields[2] = friction
    fields[3] = viscosity[...]
    fields[4] = weight[...] * mask[...].astype(F32)
    copies[0].wait()

    for pairing, out in enumerate(row_out):
        send_last = lax.axis_index("gx") % 2 == pairing
        base = pl.ds(pl.multiple_of(jnp.where(send_last, rows - PAD, 0), PAD), PAD)
        out[:PLANES] = dirs[:, base, :]
        out[PLANES:] = fields[:, base, :]

    lane = iota((8, LANES), 1)
    for g in range(rows // 8):
        span = slice(8 * g, 8 * g + 8)
        for q, (planes, count) in enumerate(((dirs, PLANES), (fields, FIELDS))):
            first = planes[0, span, :LANES]
            last = roll(planes[0, span, cols - LANES :], PAD)
            for p in range(1, count):
                here = lane >= PAD * p
                first = jnp.where(here, roll(planes[p, span, :LANES], PAD * p), first)
                last = jnp.where(
                    here, roll(planes[p, span, cols - LANES :], PAD * (p + 1)), last
                )
            for pairing, out in enumerate(col_out):
                send_last = lax.axis_index("gy") % 2 == pairing
                out[q, g] = jnp.where(send_last, last, first)
    for i in range(count_x):
        send_last = lax.axis_index("gx") % 2 == i
        base = pl.ds(jnp.where(send_last, (rows - PAD) // 8, 0), PAD // 8)
        for j in range(count_y):
            corner_out[i * count_y + j][...] = col_out[j][:, base]


def from_bands(tiles):
    block = iota((8, LANES), 1) // SPANS
    out = []
    for column in range(BANDS):
        value = tiles[0]
        for band in range(1, BANDS):
            value = jnp.where(block == (column + band) % BANDS, tiles[band], value)
        out.append(roll(value, -SPANS * column) if column else value)
    return out


def to_bands(tiles):
    block = iota((8, LANES), 1) // SPANS
    turned = [roll(tile, SPANS * column) if column else tile for column, tile in enumerate(tiles)]
    out = []
    for band in range(BANDS):
        value = turned[0]
        for column in range(1, BANDS):
            value = jnp.where(block == (column + band) % BANDS, turned[column], value)
        out.append(value)
    return out


def band_places(cols, wide):
    slot = np.arange(LANES) % PAD
    column = np.concatenate([np.arange(cols) + PAD, slot, slot + cols + PAD])
    span, j = column // wide, column % wide
    out = np.zeros((BANDS, column.size, pl.cdiv(wide, BANDS) * LANES), np.float32)
    for band in range(BANDS):
        lane = LANES * (j // BANDS) + SPANS * ((j + band) % BANDS) + span
        out[band, np.arange(column.size), lane] = 1.0
    return out.astype(BF16)


def split_dot(value, places, transposed=False):
    total = None
    for step in range(PARTS):
        part = value.astype(BF16)
        product = lax.dot_general(
            part,
            places,
            (((1,), (1 if transposed else 0,)), ((), ())),
            preferred_element_type=F32,
        )
        total = product if total is None else total + product
        if step < PARTS - 1:
            value = value - part.astype(F32)
    return total


def solve(counts, span, *refs):
    count_x, count_y = counts
    row_first, row_count = span
    got_rows, refs = refs[:count_x], refs[count_x:]
    got_cols, refs = refs[:count_y], refs[count_y:]
    got_corners, refs = refs[: count_x * count_y], refs[count_x * count_y :]
    dirs, fields, places, *refs = refs
    *outs, halo_rows, halo_cols, lined, turned, planes, coeffs, extras, base, ping, pong = refs
    rows, cols = dirs.shape[1:]
    tall = lined.shape[0]
    over = (tall - row_count) // 2
    high = tall // BANDS
    wide = planes.shape[2]
    groups = (rows + 2 * PAD) // 8
    edge = PAD // 8
    even = [lax.axis_index("gx") % 2 == 0, lax.axis_index("gy") % 2 == 0]

    def sides(axis, one, two):
        return jnp.where(even[axis], two, one), jnp.where(even[axis], one, two)

    def pair(got, index):
        one = got[0][index]
        return one, (got[1][index] if len(got) > 1 else jnp.zeros_like(one))

    for p in range(PLANES + FIELDS):
        halo_rows[0, p], halo_rows[1, p] = sides(0, *pair(got_rows, p))
    for q in range(2):
        left, right = sides(1, *pair(got_cols, q))
        halo_cols[0, q, edge : groups - edge] = left
        halo_cols[1, q, edge : groups - edge] = right
        by_x = [
            sides(1, *pair(got_corners[i * count_y : (i + 1) * count_y], q))
            for i in range(count_x)
        ]
        for side in range(2):
            one = by_x[0][side]
            two = by_x[1][side] if count_x > 1 else jnp.zeros_like(one)
            above, below = sides(0, one, two)
            halo_cols[side, q, :edge] = above
            halo_cols[side, q, groups - edge :] = below

    lanes_out = turned.shape[2]
    lane = iota((8, LANES), 1)
    own_slot = lane // PAD == iota((8, LANES), 0)

    def over_rows(body):
        for i in range(high):
            body(i)

    for q, (source, first, count) in enumerate(((dirs, 0, PLANES), (fields, PLANES, FIELDS))):
        for g in range(groups):
            lines_of = [8 * g + d - PAD - (row_first - over) for d in range(8)]
            if lines_of[-1] < 0 or lines_of[0] >= tall:
                continue
            inner = edge <= g < groups - edge
            side, at = (0, g) if g < edge else (1, g - groups + edge)
            stack = []
            for p in range(PLANES):
                if p >= count:
                    stack.append(jnp.zeros((8, cols), F32))
                elif inner:
                    stack.append(source[p, 8 * (g - edge) : 8 * (g - edge) + 8, :])
                else:
                    stack.append(halo_rows[side, first + p, 8 * at : 8 * at + 8, :])
            lines = jnp.swapaxes(jnp.stack(stack), 0, 1)
            for d, line in enumerate(lines_of):
                if 0 <= line < tall:
                    lined[line, :, :cols] = lines[d]
                    for side_y in range(2):
                        begin = cols + LANES * side_y
                        lined[line, :, begin : begin + LANES] = jnp.where(
                            own_slot, halo_cols[side_y, q, g, d : d + 1, :], 0.0
                        )

        for b in range(BANDS):
            value = lined[pl.ds(high * b, high)].reshape(high * 8, cols + 2 * LANES)
            turned[pl.ds(high * b, high)] = split_dot(value, places[b]).reshape(
                high, 8, lanes_out
            )

        def band(i):
            for t in range(lanes_out // LANES):
                tiles = [
                    turned[high * b + i, :, LANES * t : LANES * t + LANES] for b in range(BANDS)
                ]
                for j, tile in enumerate(from_bands(tiles)[: wide - BANDS * t], BANDS * t):
                    planes[q, i, j] = tile

        over_rows(band)

    row_of = iota((8, LANES), 0)
    kind = row_of % 4
    ax = jnp.where(row_of < 4, WEIGHTS[0][0], WEIGHTS[1][0])
    ay = jnp.where(row_of < 4, WEIGHTS[0][1], WEIGHTS[1][1])
    along = jnp.where(kind < 2, ax, ay)

    def weigh(i, above, below, turn_above, turn_below):
        def field(k, row, j):
            return jnp.broadcast_to(planes[1, row, j, k : k + 1, :], (8, LANES))

        mids = [field(3, i, j) for j in range(wide)]
        wests = [roll(mids[-1], 1)] + mids[:-1]
        easts = mids[1:] + [roll(mids[0], -1)]
        for j in range(wide):
            mid = mids[j]
            up, down = field(3, above, j), field(3, below, j)
            up = roll(up, SPANS) if turn_above else up
            down = roll(down, -SPANS) if turn_below else down
            east, west = 0.5 * (mid + down), 0.5 * (mid + up)
            north, south = 0.5 * (mid + easts[j]), 0.5 * (mid + wests[j])
            along_x, along_y = east + west, north + south
            friction, kept = field(2, i, j), field(4, i, j)

            diagonal = ax * along_x + ay * along_y + friction
            gain = jnp.where(kept != 0.0, damping / diagonal, 0.0)
            face = jnp.where(
                kind < 2,
                jnp.where(kind == 0, east, west),
                jnp.where(kind == 2, north, south),
            )
            weight = gain * along * face
            coeffs[0, i, j] = weight * (1.0 / GROWN)
            coeffs[1, i, j] = weight * (1.0 / KEEP_BACK)
            coeffs[2, i, j] = weight * (-1.0 / SHRUNK)
            pull = jnp.where(row_of < 4, field(0, i, j), field(1, i, j))
            extras[i, j] = jnp.where(
                kind == 1,
                GROWN * gain * kept,
                jnp.where(kind == 0, gain, GROWN) * -pull,
            )

    weigh(0, high - 1, 1, True, False)
    weigh(high - 1, high - 2, 0, False, True)

    def weigh_inner(i, _):
        weigh(i, i - 1, i + 1, False, False)
        return 0

    lax.fori_loop(1, high - 1, weigh_inner, 0, unroll=4)

    def put(ref, m, i, j, value, edges=True):
        ref[m, i + 1, j] = value
        if edges and isinstance(i, int):
            if i == 0:
                ref[m, high + 1, j] = roll(value, -SPANS)
            if i == high - 1:
                ref[m, 0, j] = roll(value, SPANS)

    def extra(kind, m, i, j):
        return extras[i, j, pl.ds(4 * m + kind, 1), :]

    def start(i):
        for j in range(wide):
            for m in range(2):
                put(base, m, i, j, extra(0, m, i, j) * planes[0, i, j])

    over_rows(start)

    def sweep(source, scale, store):
        def body(i):
            for m in range(2):
                mids = [source[m, i + 1, j] for j in range(wide)]
                before = [roll(mids[-1], 1)] + mids[:-1]
                after = mids[1:] + [roll(mids[0], -1)]
                for j in range(wide):
                    e, w, n, s = (
                        coeffs[scale, i, j, 4 * m + d : 4 * m + d + 1, :] for d in range(4)
                    )
                    along_x = e * source[m, i + 2, j] + w * source[m, i, j]
                    along_y = n * after[j] + s * before[j]
                    store(m, i, j, mids[j] + (along_x + along_y))

        over_rows(body)

    def to(ref):
        return lambda m, i, j, value: put(ref, m, i, j, value)

    def solve_from_base(kind, _):
        sweep(base, 0, to(ping))
        sweep(ping, 1, to(pong))

        def add(m, i, j, value):
            put(base, m, i, j, ping[m, i + 1, j] + (KEEP_BACK * GROWN) * value)

        sweep(pong, 0, add)
        sweep(base, 1, to(pong))

        def last(m, i, j, value):
            value = base[m, i + 1, j] - (KEEP_BACK * SHRUNK) * value
            put(base, m, i, j, extra(kind, m, i, j) * value)

        sweep(pong, 2, last)
        return 0

    lax.fori_loop(1, 3, solve_from_base, 0)

    def unband(i):
        for t in range(lanes_out // LANES):
            columns = range(BANDS * t, min(BANDS * t + BANDS, wide))
            tiles = [base[0, i + 1, j] + base[1, i + 1, j] for j in columns]
            tiles += [jnp.zeros((8, LANES), F32)] * (BANDS - len(tiles))
            for b, tile in enumerate(to_bands(tiles)):
                turned[high * b + i, :, LANES * t : LANES * t + LANES] = tile

    over_rows(unband)

    for b in range(BANDS):
        value = turned[pl.ds(high * b, high)].reshape(high * 8, lanes_out)
        value = split_dot(value, places[b, :cols, :], transposed=True)
        lined[pl.ds(high * b, high), :, :cols] = value.reshape(high, 8, cols)

    part = row_count // len(outs)
    for k, out in enumerate(outs):
        out[...] = lined[pl.ds(over + part * (lax.axis_index("dir") ^ k), part), :, :cols]


def halves(value):
    high = value.astype(BF16)
    return high, (value - high.astype(F32)).astype(BF16)


def gram_sum(parts):
    total = cross = None
    dims = (((1,), (1,)), ((), ()))
    for r in range(parts[0].shape[0]):
        high, low = halves(jnp.concatenate([part[r] for part in parts], axis=0))
        one = lax.dot_general(high, high, dims, preferred_element_type=F32)
        two = lax.dot_general(high, low, dims, preferred_element_type=F32)
        total = one if total is None else total + one
        cross = two if cross is None else cross + two
    return total + (cross + cross.T)


def gram_first(*refs):
    refs[-1][...] = gram_sum(refs[:-1])


def by_device(value, me, held):
    for k in range(value.shape[0] // 8):
        held[pl.ds(pl.multiple_of(8 * (me ^ k), 8), 8), :] = value[8 * k : 8 * k + 8]
    return held[...]


def gram_rest(before, *refs):
    parts, (gram, held) = refs[:-2], refs[-2:]
    total = before[...] + gram_sum(parts)
    for _ in range(2):
        total = by_device(total, lax.axis_index("dir"), held).T
    gram[...] = total


def factor(gram, size):
    lane = iota((size, LANES), 1)
    row_of = iota((size, LANES), 0)
    wide = jnp.concatenate([gram, jnp.zeros((size, LANES - size), F32)], axis=1)
    work = jnp.where(lane < size, wide, jnp.where(lane == row_of + size, 1.0, 0.0))
    pivots = jnp.ones((size, 1), F32)
    index = iota((size, 1), 0)
    for k in range(size):
        top = work[k : k + 1, :]
        pivot = top[:, k : k + 1]
        ratio = jnp.where(index > k, work[:, k : k + 1] / pivot, 0.0)
        pivots = jnp.where(index == k, pivot, pivots)
        work = work - ratio * top
    return work / jnp.sqrt(pivots), lane, row_of


def basis_of(cells, pieces, terms, *refs):
    sums, refs = refs[:terms], refs[terms:]
    own, refs = refs[: 4 * pieces], refs[4 * pieces :]
    *outs, upper, held = refs
    count = len(outs)
    size = sums[0].shape[0]
    gram = functools.reduce(lambda a, b: a + b, [term[...] for term in sums])
    work, lane, row_of = factor(gram / cells, size)
    upper[...] = jnp.where(lane >= row_of, work, 0.0)[:, :size]
    inverse = work[:, size : 2 * size]
    for _ in range(2):
        inverse = by_device(inverse, lax.axis_index("dir"), held).T
    high, low = halves(inverse)
    both = jnp.concatenate([high, low], axis=0)
    base = 0
    for piece in range(pieces):
        parts = own[count * piece : count * piece + count]
        for r in range(parts[0].shape[0]):
            value = jnp.concatenate([part[r] for part in parts], axis=0)
            value_high, value_low = halves(value)
            first = jnp.dot(both, value_high, preferred_element_type=F32)
            second = jnp.dot(high, value_low, preferred_element_type=F32)
            total = first[:size] + (first[size:] + second)
            for k, out in enumerate(outs):
                out[base + r] = total[8 * k : 8 * k + 8]
        base += parts[0].shape[0]


def assemble(spans, *refs):
    parts, (out, held) = refs[:-2], refs[-2:]
    count = len(parts)
    base = 0
    for first, rows in spans:
        share = rows // count
        for k, part in enumerate(parts):
            at = first + share * (lax.axis_index("dir") ^ k)
            held[pl.ds(at, share)] = part[base : base + share]
        base += share
    for g in range(out.shape[1] // 8):
        out[:, 8 * g : 8 * g + 8, :] = jnp.swapaxes(held[8 * g : 8 * g + 8], 0, 1)


def call(kernel, outs, *args, scratch=(), limit=8, space=pltpu.VMEM):
    vmem = pl.BlockSpec(memory_space=pltpu.VMEM)
    shapes = [jax.ShapeDtypeStruct(shape, F32) for shape in outs]
    return pl.pallas_call(
        kernel,
        out_shape=shapes,
        in_specs=[pl.BlockSpec(memory_space=space)] * len(args),
        out_specs=[vmem] * len(shapes),
        scratch_shapes=[
            pltpu.VMEM(shape, F32) if isinstance(shape, tuple) else shape for shape in scratch
        ],
        compiler_params=pltpu.CompilerParams(vmem_limit_bytes=limit << 20),
    )(*args)


def pairings(count):
    sets = []
    for first in (0, 1):
        pairs = [(i, i + 1) for i in range(first, count - 1, 2)]
        if pairs:
            sets.append(pairs + [(j, i) for i, j in pairs])
    return sets


def swap_bit(value, axis, bit):
    count = lax.axis_size(axis)
    return lax.ppermute(value, axis, [(i, i ^ bit) for i in range(count)])


def partial_sums(value):
    axes = ("gx", "gy", "dir")
    sizes = [lax.axis_size(axis) for axis in axes]
    strides = [sizes[1] * sizes[2], sizes[2], 1]
    bits = [
        [stride << b for b in range(size.bit_length() - 1)] for size, stride in zip(sizes, strides)
    ]
    rest = bits[1][1:] + bits[0]
    stages = [bits[2], bits[1][:1]] + [rest[i : i + 2] for i in range(0, len(rest), 2)]
    count = sizes[0] * strides[0]
    terms = [value]
    for stage in stages:
        value = functools.reduce(lambda a, b: a + b, terms)
        masks = [0]
        for bit in stage:
            masks += [mask | bit for mask in masks]
        terms = [value] + [
            lax.ppermute(value, axes, [(i, i ^ mask) for i in range(count)]) for mask in masks[1:]
        ]
    return terms


def on_device(directions, velocity, viscosity, basal_drag, misfit_weight, ice_mask, grounded):
    own, rows, cols = directions.shape
    across = lax.axis_size("dir")
    args = (directions, velocity, viscosity, basal_drag, misfit_weight, ice_mask, grounded)

    count_y = lax.axis_size("gy")
    sets_x, sets_y = pairings(lax.axis_size("gx")), pairings(count_y)
    counts = (len(sets_x), len(sets_y))
    fields, *messages = call(
        functools.partial(pack, counts),
        [(FIELDS, rows, cols)]
        + [(PLANES + FIELDS, PAD, cols)] * counts[0]
        + [(2, rows // 8, 8, LANES)] * counts[1]
        + [(2, PAD // 8, 8, LANES)] * (counts[0] * counts[1]),
        *args,
        scratch=[pltpu.VMEM(a.shape, a.dtype) for a in args] + [pltpu.SemaphoreType.DMA((7,))],
        space=pl.ANY,
        limit=60,
    )
    moves = [("gx", s) for s in sets_x] + [("gy", s) for s in sets_y]
    for set_x in sets_x:
        for set_y in sets_y:
            pairs = [(a * count_y + c, b * count_y + d) for a, b in set_x for c, d in set_y]
            moves.append((("gx", "gy"), pairs))
    got = [lax.ppermute(m, axis, pairs) for m, (axis, pairs) in zip(messages, moves)]

    over = REACH + 2
    wide = pl.cdiv(cols + 2 * PAD, SPANS)
    groups = (rows + 2 * PAD) // 8
    lanes_out = pl.cdiv(wide, BANDS) * LANES
    places = band_places(cols, wide)
    spans = [(0, FIRST_ROWS * rows // 128), (FIRST_ROWS * rows // 128, rows - FIRST_ROWS * rows // 128)]
    pieces = []
    for span in spans:
        tall = span[1] + 2 * over
        high = tall // BANDS
        state = (2, high + 2, wide, 8, LANES)
        own_parts = call(
            functools.partial(solve, counts, span),
            [(span[1] // across, own, cols)] * across,
            *got,
            directions,
            fields,
            places,
            scratch=[
                (2, PLANES + FIELDS, PAD, cols),
                (2, 2, groups, 8, LANES),
                (tall, 8, cols + 2 * LANES),
                (tall, 8, lanes_out),
                (2, high, wide, 8, LANES),
                (3, high, wide, 8, LANES),
                (high, wide, 8, LANES),
                state,
                state,
                state,
            ],
            limit=32,
        )
        pieces.append(
            [own_parts[0]] + [swap_bit(own_parts[k], "dir", k) for k in range(1, across)]
        )
    total = own * across
    (gram,) = call(gram_first, [(total, total)], *pieces[0])
    (gram,) = call(
        gram_rest, [(total, total)], gram, *pieces[1], scratch=[(total, total)]
    )
    grams = partial_sums(gram)
    count = rows * cols * lax.axis_size("gx") * lax.axis_size("gy")
    *parts, upper = call(
        functools.partial(basis_of, float(count), len(pieces), len(grams)),
        [(rows // across, own, cols)] * across + [(total, total)],
        *grams,
        *pieces[0],
        *pieces[1],
        scratch=[(total, total)],
    )
    parts = [parts[0]] + [swap_bit(parts[k], "dir", k) for k in range(1, across)]
    (basis,) = call(
        functools.partial(assemble, spans),
        [(own, rows, cols)],
        *parts,
        scratch=[(rows, own, cols)],
    )
    return (basis, upper)


def solution(mesh):
    tile = P("gx", "gy")
    placed = (P("dir", "gx", "gy"), P(None, "gx", "gy")) + (tile,) * 5
    return jax.shard_map(
        on_device,
        mesh=mesh,
        in_specs=placed,
        out_specs=(P("dir", "gx", "gy"), P()),
        check_vma=False,
    )
```

```python
import functools

import jax
import jax.numpy as jnp
from jax import lax
from jax.experimental import pallas as pl
from jax.experimental.pallas import tpu as pltpu
from jax.sharding import PartitionSpec as P

SWEEPS = 6
damping = 0.8
KEEP_BACK = 1.0 - damping
GROWN, SHRUNK = 1.0 + KEEP_BACK, 1.0 - KEEP_BACK
REACH = 2 * (SWEEPS - 1)
PAD = 16
LANES = 128
BANDS = 4
SPANS = LANES // BANDS
PLANES = 8
SWAPS = (0, 2, 3, 1)
FIELDS = 5
F32 = jnp.float32
BF16 = jnp.bfloat16
WEIGHTS = ((4.0, 1.0), (1.0, 4.0))
PARTS = 2
FIRST_ROWS = 88


def iota(shape, dim):
    return lax.broadcasted_iota(jnp.int32, shape, dim)


def roll(value, shift):
    return pltpu.roll(value, shift % LANES, 1)


def put_fields(out, velocity, viscosity, drag, weight, mask, grounded):
    friction = drag[...] * grounded[...].astype(F32)
    out[0] = friction * velocity[0]
    out[1] = friction * velocity[1]
    out[2] = friction
    out[3] = viscosity[...]
    out[4] = weight[...] * mask[...].astype(F32)


def pack(counts, *refs):
    count_x, count_y = counts
    sources, refs = refs[:7], refs[7:]
    fields, refs = refs[0], refs[1:]
    row_out, refs = refs[:count_x], refs[count_x:]
    col_out, refs = refs[:count_y], refs[count_y:]
    corner_out, refs = refs[: count_x * count_y], refs[count_x * count_y :]
    held, dirs, sems = refs[:6], *refs[6:]
    copies = [
        pltpu.make_async_copy(source, target, sems.at[i])
        for i, (source, target) in enumerate(zip(sources[1:], held))
    ]
    late = [
        pltpu.make_async_copy(sources[0].at[p], dirs.at[p], sems.at[len(copies) + p])
        for p in range(PLANES)
    ]
    for copy in copies + late:
        copy.start()
    for copy in copies:
        copy.wait()
    rows, cols = dirs.shape[1:]
    put_fields(fields, *held)
    for copy in late:
        copy.wait()

    for pairing, out in enumerate(row_out):
        send_last = lax.axis_index("gx") % 2 == pairing
        base = pl.ds(pl.multiple_of(jnp.where(send_last, rows - PAD, 0), PAD), PAD)
        out[:PLANES] = dirs[:, base, :]
        out[PLANES:] = fields[:, base, :]

    lane = iota((8, LANES), 1)
    for g in range(rows // 8):
        span = slice(8 * g, 8 * g + 8)
        for q, (planes, count) in enumerate(((dirs, PLANES), (fields, FIELDS))):
            first = planes[0, span, :LANES]
            last = roll(planes[0, span, cols - LANES :], PAD)
            for p in range(1, count):
                here = lane >= PAD * p
                first = jnp.where(here, roll(planes[p, span, :LANES], PAD * p), first)
                last = jnp.where(
                    here, roll(planes[p, span, cols - LANES :], PAD * (p + 1)), last
                )
            for pairing, out in enumerate(col_out):
                send_last = lax.axis_index("gy") % 2 == pairing
                out[q, g] = jnp.where(send_last, last, first)
    for i in range(count_x):
        send_last = lax.axis_index("gx") % 2 == i
        base = pl.ds(jnp.where(send_last, (rows - PAD) // 8, 0), PAD // 8)
        for j in range(count_y):
            corner_out[i * count_y + j][...] = col_out[j][:, base]


def from_bands(tiles):
    block = iota((8, LANES), 1) // SPANS
    out = []
    for column in range(BANDS):
        value = tiles[0]
        for band in range(1, BANDS):
            value = jnp.where(block == (column + band) % BANDS, tiles[band], value)
        out.append(roll(value, -SPANS * column) if column else value)
    return out


def to_bands(tiles):
    block = iota((8, LANES), 1) // SPANS
    turned = [roll(tile, SPANS * column) if column else tile for column, tile in enumerate(tiles)]
    out = []
    for band in range(BANDS):
        value = turned[0]
        for column in range(1, BANDS):
            value = jnp.where(block == (column + band) % BANDS, turned[column], value)
        out.append(value)
    return out


def line_up(dirs, fields, lines, places):
    rows, cols = dirs.shape[1:]
    for g in range(rows // 8):
        at = slice(8 * g, 8 * g + 8)
        lines[at, :PLANES, :] = jnp.swapaxes(dirs[:, at, :], 0, 1)
        stack = [fields[k, at, :] for k in range(FIELDS)]
        stack += [jnp.zeros((8, cols), F32)] * (PLANES - FIELDS)
        lines[at, PLANES:, :] = jnp.swapaxes(jnp.stack(stack), 0, 1)
    wide = pl.cdiv(cols + 2 * PAD, SPANS)
    k, lane = (iota(places.shape[1:], dim) for dim in (0, 1))
    slot = k % PAD + jnp.where(k < cols + LANES, 0, cols + PAD)
    column = jnp.where(k < cols, k + PAD, slot)
    tile, block, span = lane // LANES, (lane // SPANS) % BANDS, lane % SPANS
    for band in range(BANDS):
        j = BANDS * tile + (block + BANDS - band) % BANDS
        here = (column == wide * span + j) & (j < wide)
        places[band] = jnp.where(here, 1.0, 0.0).astype(BF16)


def split_dot(value, places, transposed=False):
    total = None
    for step in range(PARTS):
        part = value.astype(BF16)
        product = lax.dot_general(
            part,
            places,
            (((1,), (1 if transposed else 0,)), ((), ())),
            preferred_element_type=F32,
        )
        total = product if total is None else total + product
        if step < PARTS - 1:
            value = value - part.astype(F32)
    return total


def solve(counts, span, *refs):
    count_x, count_y = counts
    row_first, row_count = span
    got_rows, refs = refs[:count_x], refs[count_x:]
    got_cols, refs = refs[:count_y], refs[count_y:]
    got_corners, refs = refs[: count_x * count_y], refs[count_x * count_y :]
    own_lines, places, *refs = refs
    *outs, halo_rows, halo_cols, lined, turned, planes, coeffs, extras, base, ping, pong = refs
    rows, _, cols = own_lines.shape
    tall = lined.shape[0]
    over = (tall - row_count) // 2
    high = tall // BANDS
    wide = planes.shape[2]
    groups = (rows + 2 * PAD) // 8
    edge = PAD // 8
    even = [lax.axis_index("gx") % 2 == 0, lax.axis_index("gy") % 2 == 0]

    def sides(axis, one, two):
        return jnp.where(even[axis], two, one), jnp.where(even[axis], one, two)

    def pair(got, index):
        one = got[0][index]
        return one, (got[1][index] if len(got) > 1 else jnp.zeros_like(one))

    for p in range(PLANES + FIELDS):
        halo_rows[0, p], halo_rows[1, p] = sides(0, *pair(got_rows, p))
    for q in range(2):
        left, right = sides(1, *pair(got_cols, q))
        halo_cols[0, q, edge : groups - edge] = left
        halo_cols[1, q, edge : groups - edge] = right
        by_x = [
            sides(1, *pair(got_corners[i * count_y : (i + 1) * count_y], q))
            for i in range(count_x)
        ]
        for side in range(2):
            one = by_x[0][side]
            two = by_x[1][side] if count_x > 1 else jnp.zeros_like(one)
            above, below = sides(0, one, two)
            halo_cols[side, q, :edge] = above
            halo_cols[side, q, groups - edge :] = below

    lanes_out = turned.shape[2]
    lane = iota((8, LANES), 1)
    own_slot = lane // PAD == iota((8, LANES), 0)

    def over_rows(body):
        for i in range(high):
            body(i)

    for q, (first, count) in enumerate(((0, PLANES), (PLANES, FIELDS))):
        for g in range(groups):
            lines_of = [8 * g + d - PAD - (row_first - over) for d in range(8)]
            if lines_of[-1] < 0 or lines_of[0] >= tall:
                continue
            inner = edge <= g < groups - edge
            if not inner:
                side, at = (0, g) if g < edge else (1, g - groups + edge)
                stack = [
                    halo_rows[side, first + p, 8 * at : 8 * at + 8, :] for p in range(count)
                ]
                stack += [jnp.zeros((8, cols), F32)] * (PLANES - count)
                lines = jnp.swapaxes(jnp.stack(stack), 0, 1)
            for d, line in enumerate(lines_of):
                if 0 <= line < tall:
                    lined[line, :, :cols] = (
                        own_lines[8 * (g - edge) + d, PLANES * q : PLANES * q + PLANES, :]
                        if inner
                        else lines[d]
                    )
                    for side_y in range(2):
                        begin = cols + LANES * side_y
                        lined[line, :, begin : begin + LANES] = jnp.where(
                            own_slot, halo_cols[side_y, q, g, d : d + 1, :], 0.0
                        )

        for b in range(BANDS):
            value = lined[pl.ds(high * b, high)].reshape(high * 8, cols + 2 * LANES)
            turned[pl.ds(high * b, high)] = split_dot(value, places[b]).reshape(
                high, 8, lanes_out
            )

        def band(i):
            for t in range(lanes_out // LANES):
                tiles = [
                    turned[high * b + i, :, LANES * t : LANES * t + LANES] for b in range(BANDS)
                ]
                for j, tile in enumerate(from_bands(tiles)[: wide - BANDS * t], BANDS * t):
                    planes[q, i, j] = tile

        over_rows(band)

    row_of = iota((8, LANES), 0)
    kind = row_of % 4
    ax = jnp.where(row_of < 4, WEIGHTS[0][0], WEIGHTS[1][0])
    ay = jnp.where(row_of < 4, WEIGHTS[0][1], WEIGHTS[1][1])
    along = jnp.where(kind < 2, ax, ay)

    def weigh(i, above, below, turn_above, turn_below):
        def field(k, row, j):
            return jnp.broadcast_to(planes[1, row, j, k : k + 1, :], (8, LANES))

        mids = [field(3, i, j) for j in range(wide)]
        wests = [roll(mids[-1], 1)] + mids[:-1]
        easts = mids[1:] + [roll(mids[0], -1)]
        for j in range(wide):
            mid = mids[j]
            up, down = field(3, above, j), field(3, below, j)
            up = roll(up, SPANS) if turn_above else up
            down = roll(down, -SPANS) if turn_below else down
            east, west = 0.5 * (mid + down), 0.5 * (mid + up)
            north, south = 0.5 * (mid + easts[j]), 0.5 * (mid + wests[j])
            along_x, along_y = east + west, north + south
            friction, kept = field(2, i, j), field(4, i, j)

            diagonal = ax * along_x + ay * along_y + friction
            gain = jnp.where(kept != 0.0, damping / diagonal, 0.0)
            face = jnp.where(
                kind < 2,
                jnp.where(kind == 0, east, west),
                jnp.where(kind == 2, north, south),
            )
            weight = gain * along * face
            coeffs[0, i, j] = weight * (1.0 / GROWN)
            coeffs[1, i, j] = weight * (1.0 / KEEP_BACK)
            coeffs[2, i, j] = weight * (-1.0 / SHRUNK)
            pull = jnp.where(row_of < 4, field(0, i, j), field(1, i, j))
            extras[i, j] = jnp.where(
                kind == 1,
                GROWN * gain * kept,
                jnp.where(kind == 0, gain, GROWN) * -pull,
            )

    weigh(0, high - 1, 1, True, False)
    weigh(high - 1, high - 2, 0, False, True)

    def weigh_inner(i, _):
        weigh(i, i - 1, i + 1, False, False)
        return 0

    lax.fori_loop(1, high - 1, weigh_inner, 0, unroll=2)

    def put(ref, m, i, j, value, edges=True):
        ref[m, i + 1, j] = value
        if edges and isinstance(i, int):
            if i == 0:
                ref[m, high + 1, j] = roll(value, -SPANS)
            if i == high - 1:
                ref[m, 0, j] = roll(value, SPANS)

    def extra(kind, m, i, j):
        return extras[i, j, pl.ds(4 * m + kind, 1), :]

    def start(i):
        for j in range(wide):
            for m in range(2):
                put(base, m, i, j, extra(0, m, i, j) * planes[0, i, j])

    over_rows(start)

    def sweep(source, scale, store):
        for m in range(2):
            above, mids = ([source[m, i, j] for j in range(wide)] for i in range(2))
            for i in range(high):
                below = [source[m, i + 2, j] for j in range(wide)]
                before = [roll(mids[-1], 1)] + mids[:-1]
                after = mids[1:] + [roll(mids[0], -1)]
                for j in range(wide):
                    e, w, n, s = (
                        coeffs[scale, i, j, 4 * m + d : 4 * m + d + 1, :] for d in range(4)
                    )
                    along_x = e * below[j] + w * above[j]
                    along_y = n * after[j] + s * before[j]
                    store(m, i, j, mids[j] + (along_x + along_y))
                above, mids = mids, below

    def to(ref):
        return lambda m, i, j, value: put(ref, m, i, j, value)

    def solve_from_base(kind, _):
        sweep(base, 0, to(ping))
        sweep(ping, 1, to(pong))

        def add(m, i, j, value):
            put(base, m, i, j, ping[m, i + 1, j] + (KEEP_BACK * GROWN) * value)

        sweep(pong, 0, add)
        sweep(base, 1, to(pong))

        def last(m, i, j, value):
            value = base[m, i + 1, j] - (KEEP_BACK * SHRUNK) * value
            put(base, m, i, j, extra(kind, m, i, j) * value)

        sweep(pong, 2, last)
        return 0

    lax.fori_loop(1, 3, solve_from_base, 0)

    def unband(i):
        for t in range(lanes_out // LANES):
            columns = range(BANDS * t, min(BANDS * t + BANDS, wide))
            tiles = [base[0, i + 1, j] + base[1, i + 1, j] for j in columns]
            tiles += [jnp.zeros((8, LANES), F32)] * (BANDS - len(tiles))
            for b, tile in enumerate(to_bands(tiles)):
                turned[high * b + i, :, LANES * t : LANES * t + LANES] = tile

    over_rows(unband)

    for b in range(BANDS):
        value = turned[pl.ds(high * b, high)].reshape(high * 8, lanes_out)
        value = split_dot(value, places[b, :cols, :], transposed=True)
        lined[pl.ds(high * b, high), :, :cols] = value.reshape(high, 8, cols)

    part = row_count // len(outs)
    for k, out in zip(SWAPS, outs):
        out[...] = lined[pl.ds(over + part * (lax.axis_index("dir") ^ k), part), :, :cols]


def halves(value):
    high = value.astype(BF16)
    return high, (value - high.astype(F32)).astype(BF16)


def gram_sum(parts):
    total = cross = None
    dims = (((1,), (1,)), ((), ()))
    for r in range(parts[0].shape[0]):
        high, low = halves(jnp.concatenate([part[r] for part in parts], axis=0))
        one = lax.dot_general(high, high, dims, preferred_element_type=F32)
        two = lax.dot_general(high, low, dims, preferred_element_type=F32)
        total = one if total is None else total + one
        cross = two if cross is None else cross + two
    return total + (cross + cross.T)


def gram_first(*refs):
    refs[-1][...] = gram_sum(refs[:-1])


def by_device(value, me, held):
    for n, k in enumerate(SWAPS):
        held[pl.ds(pl.multiple_of(8 * (me ^ k), 8), 8), :] = value[8 * n : 8 * n + 8]
    return held[...]


def to_device(value, me, held):
    held[...] = value
    blocks = [held[pl.ds(pl.multiple_of(8 * (me ^ k), 8), 8), :] for k in SWAPS]
    return jnp.concatenate(blocks, axis=0)


def gram_rest(before, *refs):
    parts, (gram, held) = refs[:-2], refs[-2:]
    total = before[...] + gram_sum(parts)
    for _ in range(2):
        total = by_device(total, lax.axis_index("dir"), held).T
    gram[...] = total


def factor(gram, size):
    lane = iota((size, LANES), 1)
    row_of = iota((size, LANES), 0)
    wide = jnp.concatenate([gram, jnp.zeros((size, LANES - size), F32)], axis=1)
    work = jnp.where(lane < size, wide, jnp.where(lane == row_of + size, 1.0, 0.0))
    pivots = jnp.ones((size, 1), F32)
    index = iota((size, 1), 0)
    for k in range(size):
        top = work[k : k + 1, :]
        pivot = top[:, k : k + 1]
        ratio = jnp.where(index > k, work[:, k : k + 1] / pivot, 0.0)
        pivots = jnp.where(index == k, pivot, pivots)
        work = work - ratio * top
    return work / jnp.sqrt(pivots), lane, row_of


def form_basis(inverse, pieces, outs):
    count = len(SWAPS)
    high, low = halves(inverse)
    both = jnp.concatenate([high, low], axis=0)
    size = inverse.shape[0]
    base = 0
    for piece in range(len(pieces) // count):
        parts = pieces[count * piece : count * piece + count]
        for r in range(parts[0].shape[0]):
            value_high, value_low = halves(jnp.concatenate([part[r] for part in parts], axis=0))
            first = jnp.dot(both, value_high, preferred_element_type=F32)
            second = jnp.dot(high, value_low, preferred_element_type=F32)
            total = first[:size] + (first[size:] + second)
            for n, out in enumerate(outs):
                out[base + r] = total[8 * n : 8 * n + 8]
        base += parts[0].shape[0]


def basis_of(cells, terms, *refs):
    sums, refs = refs[:terms], refs[terms:]
    count = len(SWAPS)
    pieces, outs, (upper, held) = refs[: -count - 2], refs[-count - 2 : -2], refs[-2:]
    size = sums[0].shape[0]
    gram = functools.reduce(lambda a, b: a + b, [term[...] for term in sums])
    work, lane, row_of = factor(gram / cells, size)
    upper[...] = jnp.where(lane >= row_of, work, 0.0)[:, :size]
    value = work[:, size : 2 * size]
    for _ in range(2):
        value = to_device(value, lax.axis_index("dir"), held).T
    form_basis(value, pieces, outs)


def assemble(spans, *refs):
    parts, (out, held) = refs[:-2], refs[-2:]
    count = len(parts)
    base = 0
    for first, rows in spans:
        share = rows // count
        for k, part in zip(SWAPS, parts):
            at = first + share * (lax.axis_index("dir") ^ k)
            held[pl.ds(at, share)] = part[base : base + share]
        base += share
    for g in range(out.shape[1] // 8):
        out[:, 8 * g : 8 * g + 8, :] = jnp.swapaxes(held[8 * g : 8 * g + 8], 0, 1)


def call(kernel, outs, *args, scratch=(), limit=8, space=pltpu.VMEM):
    vmem = pl.BlockSpec(memory_space=pltpu.VMEM)
    shapes = [
        jax.ShapeDtypeStruct(shape, F32) if isinstance(shape, tuple) else shape for shape in outs
    ]
    return pl.pallas_call(
        kernel,
        out_shape=shapes,
        in_specs=[pl.BlockSpec(memory_space=space)] * len(args),
        out_specs=[vmem] * len(shapes),
        scratch_shapes=[
            pltpu.VMEM(shape, F32) if isinstance(shape, tuple) else shape for shape in scratch
        ],
        compiler_params=pltpu.CompilerParams(vmem_limit_bytes=limit << 20),
    )(*args)


def pairings(count):
    sets = []
    for first in (0, 1):
        pairs = [(i, i + 1) for i in range(first, count - 1, 2)]
        if pairs:
            sets.append(pairs + [(j, i) for i, j in pairs])
    return sets


def swap_bit(value, axis, bit):
    count = lax.axis_size(axis)
    return lax.ppermute(value, axis, [(i, i ^ bit) for i in range(count)])


def partial_sums(value):
    axes = ("gx", "gy", "dir")
    sizes = [lax.axis_size(axis) for axis in axes]
    strides = [sizes[1] * sizes[2], sizes[2], 1]
    bits = [
        [stride << b for b in range(size.bit_length() - 1)] for size, stride in zip(sizes, strides)
    ]
    rest = bits[1][1:] + bits[0]
    stages = [bits[2], bits[1][:1]] + [rest[i : i + 2] for i in range(0, len(rest), 2)]
    count = sizes[0] * strides[0]
    terms = [value]
    for stage in stages:
        value = functools.reduce(lambda a, b: a + b, terms)
        masks = [0]
        for bit in stage:
            masks += [mask | bit for mask in masks]
        terms = [value] + [
            lax.ppermute(value, axes, [(i, i ^ mask) for i in range(count)]) for mask in masks[1:]
        ]
    return terms


def on_device(directions, velocity, viscosity, basal_drag, misfit_weight, ice_mask, grounded):
    own, rows, cols = directions.shape
    across = lax.axis_size("dir")
    args = (directions, velocity, viscosity, basal_drag, misfit_weight, ice_mask, grounded)

    count_y = lax.axis_size("gy")
    sets_x, sets_y = pairings(lax.axis_size("gx")), pairings(count_y)
    counts = (len(sets_x), len(sets_y))
    fields, *messages = call(
        functools.partial(pack, counts),
        [(FIELDS, rows, cols)]
        + [(PLANES + FIELDS, PAD, cols)] * counts[0]
        + [(2, rows // 8, 8, LANES)] * counts[1]
        + [(2, PAD // 8, 8, LANES)] * (counts[0] * counts[1]),
        *args,
        scratch=[pltpu.VMEM(a.shape, a.dtype) for a in args[1:]]
        + [directions.shape]
        + [pltpu.SemaphoreType.DMA((len(args) - 1 + PLANES,))],
        space=pl.ANY,
        limit=60,
    )
    moves = [("gx", s) for s in sets_x] + [("gy", s) for s in sets_y]
    for set_x in sets_x:
        for set_y in sets_y:
            pairs = [(a * count_y + c, b * count_y + d) for a, b in set_x for c, d in set_y]
            moves.append((("gx", "gy"), pairs))
    got = [lax.ppermute(m, axis, pairs) for m, (axis, pairs) in zip(messages, moves)]

    over = REACH + 2
    wide = pl.cdiv(cols + 2 * PAD, SPANS)
    groups = (rows + 2 * PAD) // 8
    lanes_out = pl.cdiv(wide, BANDS) * LANES
    own_lines, places = call(
        line_up,
        [
            (rows, 2 * PLANES, cols),
            jax.ShapeDtypeStruct((BANDS, cols + 2 * LANES, lanes_out), BF16),
        ],
        directions,
        fields,
        limit=24,
    )
    spans = [(0, FIRST_ROWS * rows // 128), (FIRST_ROWS * rows // 128, rows - FIRST_ROWS * rows // 128)]
    pieces = []
    for span in spans:
        tall = span[1] + 2 * over
        high = tall // BANDS
        state = (2, high + 2, wide, 8, LANES)
        own_parts = call(
            functools.partial(solve, counts, span),
            [(span[1] // across, own, cols)] * across,
            *got,
            own_lines,
            places,
            scratch=[
                (2, PLANES + FIELDS, PAD, cols),
                (2, 2, groups, 8, LANES),
                (tall, 8, cols + 2 * LANES),
                (tall, 8, lanes_out),
                (2, high, wide, 8, LANES),
                (3, high, wide, 8, LANES),
                (high, wide, 8, LANES),
                state,
                state,
                state,
            ],
            limit=32,
        )
        pieces.append(
            [own_parts[0]] + [swap_bit(p, "dir", k) for p, k in zip(own_parts[1:], SWAPS[1:])]
        )
    total = own * across
    (gram,) = call(gram_first, [(total, total)], *pieces[0])
    (gram,) = call(
        gram_rest, [(total, total)], gram, *pieces[1], scratch=[(total, total)]
    )
    grams = partial_sums(gram)
    count = rows * cols * lax.axis_size("gx") * lax.axis_size("gy")
    part = (rows // across, own, cols)
    *parts, upper = call(
        functools.partial(basis_of, float(count), len(grams)),
        [part] * across + [(total, total)],
        *grams,
        *pieces[0],
        *pieces[1],
        scratch=[(total, total)],
    )
    parts = [parts[0]] + [swap_bit(p, "dir", k) for p, k in zip(parts[1:], SWAPS[1:])]
    (basis,) = call(
        functools.partial(assemble, spans),
        [(own, rows, cols)],
        *parts,
        scratch=[(rows, own, cols)],
    )
    return (basis, upper)


def solution(mesh):
    tile = P("gx", "gy")
    placed = (P("dir", "gx", "gy"), P(None, "gx", "gy")) + (tile,) * 5
    return jax.shard_map(
        on_device,
        mesh=mesh,
        in_specs=placed,
        out_specs=(P("dir", "gx", "gy"), P()),
        check_vma=False,
    )
```

```python
import functools

import jax
import jax.numpy as jnp
from jax import lax
from jax.experimental import pallas as pl
from jax.experimental.pallas import tpu as pltpu
from jax.sharding import PartitionSpec as P

SWEEPS = 6
damping = 0.8
KEEP_BACK = 1.0 - damping
GROWN, SHRUNK = 1.0 + KEEP_BACK, 1.0 - KEEP_BACK
REACH = 2 * (SWEEPS - 1)
PAD = 16
LANES = 128
BANDS = 4
SPANS = LANES // BANDS
PLANES = 8
SWAPS = (0, 2, 3, 1)
FIELDS = 5
F32 = jnp.float32
BF16 = jnp.bfloat16
WEIGHTS = ((4.0, 1.0), (1.0, 4.0))
BLOCK = 8
PARTS = 2
FIRST_ROWS = 88


def iota(shape, dim):
    return lax.broadcasted_iota(jnp.int32, shape, dim)


def roll(value, shift):
    return pltpu.roll(value, shift % LANES, 1)


def put_fields(out, velocity, viscosity, drag, weight, mask, grounded):
    friction = drag[...] * grounded[...].astype(F32)
    out[0] = friction * velocity[0]
    out[1] = friction * velocity[1]
    out[2] = friction
    out[3] = viscosity[...]
    out[4] = weight[...] * mask[...].astype(F32)


def pack(counts, *refs):
    count_x, count_y = counts
    sources, refs = refs[:7], refs[7:]
    fields, refs = refs[0], refs[1:]
    row_out, refs = refs[:count_x], refs[count_x:]
    col_out, refs = refs[:count_y], refs[count_y:]
    corner_out, refs = refs[: count_x * count_y], refs[count_x * count_y :]
    held, dirs, sems = refs[:6], *refs[6:]
    copies = [
        pltpu.make_async_copy(source, target, sems.at[i])
        for i, (source, target) in enumerate(zip(sources[1:], held))
    ]
    late = [
        pltpu.make_async_copy(sources[0].at[p], dirs.at[p], sems.at[len(copies) + p])
        for p in range(PLANES)
    ]
    for copy in copies + late:
        copy.start()
    for copy in copies:
        copy.wait()
    rows, cols = dirs.shape[1:]
    put_fields(fields, *held)
    for copy in late:
        copy.wait()

    for pairing, out in enumerate(row_out):
        send_last = lax.axis_index("gx") % 2 == pairing
        base = pl.ds(pl.multiple_of(jnp.where(send_last, rows - PAD, 0), PAD), PAD)
        out[:PLANES] = dirs[:, base, :]
        out[PLANES:] = fields[:, base, :]

    lane = iota((8, LANES), 1)
    for g in range(rows // 8):
        span = slice(8 * g, 8 * g + 8)
        for q, (planes, count) in enumerate(((dirs, PLANES), (fields, FIELDS))):
            first = planes[0, span, :LANES]
            last = roll(planes[0, span, cols - LANES :], PAD)
            for p in range(1, count):
                here = lane >= PAD * p
                first = jnp.where(here, roll(planes[p, span, :LANES], PAD * p), first)
                last = jnp.where(
                    here, roll(planes[p, span, cols - LANES :], PAD * (p + 1)), last
                )
            for pairing, out in enumerate(col_out):
                send_last = lax.axis_index("gy") % 2 == pairing
                out[q, g] = jnp.where(send_last, last, first)
    for i in range(count_x):
        send_last = lax.axis_index("gx") % 2 == i
        base = pl.ds(jnp.where(send_last, (rows - PAD) // 8, 0), PAD // 8)
        for j in range(count_y):
            corner_out[i * count_y + j][...] = col_out[j][:, base]


def from_bands(tiles):
    block = iota((8, LANES), 1) // SPANS
    out = []
    for column in range(BANDS):
        value = tiles[0]
        for band in range(1, BANDS):
            value = jnp.where(block == (column + band) % BANDS, tiles[band], value)
        out.append(roll(value, -SPANS * column) if column else value)
    return out


def to_bands(tiles):
    block = iota((8, LANES), 1) // SPANS
    turned = [roll(tile, SPANS * column) if column else tile for column, tile in enumerate(tiles)]
    out = []
    for band in range(BANDS):
        value = turned[0]
        for column in range(1, BANDS):
            value = jnp.where(block == (column + band) % BANDS, turned[column], value)
        out.append(value)
    return out


def line_up(dirs, fields, lines, places):
    rows, cols = dirs.shape[1:]
    for g in range(rows // 8):
        at = slice(8 * g, 8 * g + 8)
        lines[at, :PLANES, :] = jnp.swapaxes(dirs[:, at, :], 0, 1)
        stack = [fields[k, at, :] for k in range(FIELDS)]
        stack += [jnp.zeros((8, cols), F32)] * (PLANES - FIELDS)
        lines[at, PLANES:, :] = jnp.swapaxes(jnp.stack(stack), 0, 1)
    wide = pl.cdiv(cols + 2 * PAD, SPANS)
    k, lane = (iota(places.shape[1:], dim) for dim in (0, 1))
    slot = k % PAD + jnp.where(k < cols + LANES, 0, cols + PAD)
    column = jnp.where(k < cols, k + PAD, slot)
    tile, block, span = lane // LANES, (lane // SPANS) % BANDS, lane % SPANS
    for band in range(BANDS):
        j = BANDS * tile + (block + BANDS - band) % BANDS
        here = (column == wide * span + j) & (j < wide)
        places[band] = jnp.where(here, 1.0, 0.0).astype(BF16)


def split_dot(value, places, transposed=False):
    total = None
    for step in range(PARTS):
        part = value.astype(BF16)
        product = lax.dot_general(
            part,
            places,
            (((1,), (1 if transposed else 0,)), ((), ())),
            preferred_element_type=F32,
        )
        total = product if total is None else total + product
        if step < PARTS - 1:
            value = value - part.astype(F32)
    return total


def solve(counts, span, *refs):
    count_x, count_y = counts
    row_first, row_count = span
    got_rows, refs = refs[:count_x], refs[count_x:]
    got_cols, refs = refs[:count_y], refs[count_y:]
    got_corners, refs = refs[: count_x * count_y], refs[count_x * count_y :]
    own_lines, places, *refs = refs
    *outs, halo_rows, halo_cols, lined, turned, planes, coeffs, extras, base, ping, pong = refs
    rows, _, cols = own_lines.shape
    tall = lined.shape[0]
    over = (tall - row_count) // 2
    high = tall // BANDS
    wide = planes.shape[2]
    groups = (rows + 2 * PAD) // 8
    edge = PAD // 8
    even = [lax.axis_index("gx") % 2 == 0, lax.axis_index("gy") % 2 == 0]

    def sides(axis, one, two):
        return jnp.where(even[axis], two, one), jnp.where(even[axis], one, two)

    def pair(got, index):
        one = got[0][index]
        return one, (got[1][index] if len(got) > 1 else jnp.zeros_like(one))

    for p in range(PLANES + FIELDS):
        halo_rows[0, p], halo_rows[1, p] = sides(0, *pair(got_rows, p))
    for q in range(2):
        left, right = sides(1, *pair(got_cols, q))
        halo_cols[0, q, edge : groups - edge] = left
        halo_cols[1, q, edge : groups - edge] = right
        by_x = [
            sides(1, *pair(got_corners[i * count_y : (i + 1) * count_y], q))
            for i in range(count_x)
        ]
        for side in range(2):
            one = by_x[0][side]
            two = by_x[1][side] if count_x > 1 else jnp.zeros_like(one)
            above, below = sides(0, one, two)
            halo_cols[side, q, :edge] = above
            halo_cols[side, q, groups - edge :] = below

    lanes_out = turned.shape[2]
    lane = iota((8, LANES), 1)
    own_slot = lane // PAD == iota((8, LANES), 0)

    def over_rows(body):
        for i in range(high):
            body(i)

    for q, (first, count) in enumerate(((0, PLANES), (PLANES, FIELDS))):
        for g in range(groups):
            lines_of = [8 * g + d - PAD - (row_first - over) for d in range(8)]
            if lines_of[-1] < 0 or lines_of[0] >= tall:
                continue
            inner = edge <= g < groups - edge
            if not inner:
                side, at = (0, g) if g < edge else (1, g - groups + edge)
                stack = [
                    halo_rows[side, first + p, 8 * at : 8 * at + 8, :] for p in range(count)
                ]
                stack += [jnp.zeros((8, cols), F32)] * (PLANES - count)
                lines = jnp.swapaxes(jnp.stack(stack), 0, 1)
            for d, line in enumerate(lines_of):
                if 0 <= line < tall:
                    lined[line, :, :cols] = (
                        own_lines[8 * (g - edge) + d, PLANES * q : PLANES * q + PLANES, :]
                        if inner
                        else lines[d]
                    )
                    for side_y in range(2):
                        begin = cols + LANES * side_y
                        lined[line, :, begin : begin + LANES] = jnp.where(
                            own_slot, halo_cols[side_y, q, g, d : d + 1, :], 0.0
                        )

        for b in range(BANDS):
            value = lined[pl.ds(high * b, high)].reshape(high * 8, cols + 2 * LANES)
            turned[pl.ds(high * b, high)] = split_dot(value, places[b]).reshape(
                high, 8, lanes_out
            )

        def band(i):
            for t in range(lanes_out // LANES):
                tiles = [
                    turned[high * b + i, :, LANES * t : LANES * t + LANES] for b in range(BANDS)
                ]
                for j, tile in enumerate(from_bands(tiles)[: wide - BANDS * t], BANDS * t):
                    planes[q, i, j] = tile

        over_rows(band)

    row_of = iota((8, LANES), 0)
    kind = row_of % 4
    ax = jnp.where(row_of < 4, WEIGHTS[0][0], WEIGHTS[1][0])
    ay = jnp.where(row_of < 4, WEIGHTS[0][1], WEIGHTS[1][1])
    along = jnp.where(kind < 2, ax, ay)

    def weigh(i, above, below, turn_above, turn_below):
        def field(k, row, j):
            return jnp.broadcast_to(planes[1, row, j, k : k + 1, :], (8, LANES))

        mids = [field(3, i, j) for j in range(wide)]
        wests = [roll(mids[-1], 1)] + mids[:-1]
        easts = mids[1:] + [roll(mids[0], -1)]
        for j in range(wide):
            mid = mids[j]
            up, down = field(3, above, j), field(3, below, j)
            up = roll(up, SPANS) if turn_above else up
            down = roll(down, -SPANS) if turn_below else down
            east, west = 0.5 * (mid + down), 0.5 * (mid + up)
            north, south = 0.5 * (mid + easts[j]), 0.5 * (mid + wests[j])
            along_x, along_y = east + west, north + south
            friction, kept = field(2, i, j), field(4, i, j)

            diagonal = ax * along_x + ay * along_y + friction
            gain = jnp.where(kept != 0.0, damping / diagonal, 0.0)
            face = jnp.where(
                kind < 2,
                jnp.where(kind == 0, east, west),
                jnp.where(kind == 2, north, south),
            )
            weight = gain * along * face
            coeffs[0, i, j] = weight * (1.0 / GROWN)
            coeffs[1, i, j] = weight * (1.0 / KEEP_BACK)
            coeffs[2, i, j] = weight * (-1.0 / SHRUNK)
            pull = jnp.where(row_of < 4, field(0, i, j), field(1, i, j))
            extras[i, j] = jnp.where(
                kind == 1,
                GROWN * gain * kept,
                jnp.where(kind == 0, gain, GROWN) * -pull,
            )

    weigh(0, high - 1, 1, True, False)
    weigh(high - 1, high - 2, 0, False, True)

    def weigh_inner(i, _):
        weigh(i, i - 1, i + 1, False, False)
        return 0

    lax.fori_loop(1, high - 1, weigh_inner, 0, unroll=2)

    def put(ref, m, i, j, value, edges=True):
        ref[m, i + 1, j] = value
        if edges and isinstance(i, int):
            if i == 0:
                ref[m, high + 1, j] = roll(value, -SPANS)
            if i == high - 1:
                ref[m, 0, j] = roll(value, SPANS)

    def extra(kind, m, i, j):
        return extras[i, j, pl.ds(4 * m + kind, 1), :]

    def start(i):
        for j in range(wide):
            for m in range(2):
                put(base, m, i, j, extra(0, m, i, j) * planes[0, i, j])

    over_rows(start)

    def sweep(source, scale, store):
        for m in range(2):
            above, mids = ([source[m, i, j] for j in range(wide)] for i in range(2))
            for i in range(high):
                below = [source[m, i + 2, j] for j in range(wide)]
                before = [roll(mids[-1], 1)] + mids[:-1]
                after = mids[1:] + [roll(mids[0], -1)]
                for j in range(wide):
                    e, w, n, s = (
                        coeffs[scale, i, j, 4 * m + d : 4 * m + d + 1, :] for d in range(4)
                    )
                    along_x = e * below[j] + w * above[j]
                    along_y = n * after[j] + s * before[j]
                    store(m, i, j, mids[j] + (along_x + along_y))
                above, mids = mids, below

    def to(ref):
        return lambda m, i, j, value: put(ref, m, i, j, value)

    def solve_from_base(kind, _):
        sweep(base, 0, to(ping))
        sweep(ping, 1, to(pong))

        def add(m, i, j, value):
            put(base, m, i, j, ping[m, i + 1, j] + (KEEP_BACK * GROWN) * value)

        sweep(pong, 0, add)
        sweep(base, 1, to(pong))

        def last(m, i, j, value):
            value = base[m, i + 1, j] - (KEEP_BACK * SHRUNK) * value
            put(base, m, i, j, extra(kind, m, i, j) * value)

        sweep(pong, 2, last)
        return 0

    lax.fori_loop(1, 3, solve_from_base, 0)

    def unband(i):
        for t in range(lanes_out // LANES):
            columns = range(BANDS * t, min(BANDS * t + BANDS, wide))
            tiles = [base[0, i + 1, j] + base[1, i + 1, j] for j in columns]
            tiles += [jnp.zeros((8, LANES), F32)] * (BANDS - len(tiles))
            for b, tile in enumerate(to_bands(tiles)):
                turned[high * b + i, :, LANES * t : LANES * t + LANES] = tile

    over_rows(unband)

    for b in range(BANDS):
        value = turned[pl.ds(high * b, high)].reshape(high * 8, lanes_out)
        value = split_dot(value, places[b, :cols, :], transposed=True)
        lined[pl.ds(high * b, high), :, :cols] = value.reshape(high, 8, cols)

    part = row_count // len(outs)
    for k, out in zip(SWAPS, outs):
        out[...] = lined[pl.ds(over + part * (lax.axis_index("dir") ^ k), part), :, :cols]


def halves(value):
    high = value.astype(BF16)
    return high, (value - high.astype(F32)).astype(BF16)


def gram_sum(parts):
    total = cross = None
    dims = (((1,), (1,)), ((), ()))
    for r in range(parts[0].shape[0]):
        high, low = halves(jnp.concatenate([part[r] for part in parts], axis=0))
        one = lax.dot_general(high, high, dims, preferred_element_type=F32)
        two = lax.dot_general(high, low, dims, preferred_element_type=F32)
        total = one if total is None else total + one
        cross = two if cross is None else cross + two
    return total + (cross + cross.T)


def gram_first(*refs):
    refs[-1][...] = gram_sum(refs[:-1])


def by_device(value, me, held):
    for n, k in enumerate(SWAPS):
        held[pl.ds(pl.multiple_of(8 * (me ^ k), 8), 8), :] = value[8 * n : 8 * n + 8]
    return held[...]


def to_device(value, me, held):
    held[...] = value
    blocks = [held[pl.ds(pl.multiple_of(8 * (me ^ k), 8), 8), :] for k in SWAPS]
    return jnp.concatenate(blocks, axis=0)


def gram_rest(before, *refs):
    parts, (gram, held) = refs[:-2], refs[-2:]
    total = before[...] + gram_sum(parts)
    for _ in range(2):
        total = by_device(total, lax.axis_index("dir"), held).T
    gram[...] = total


def factor(gram, size):
    lane = iota((size, LANES), 1)
    row_of = iota((size, LANES), 0)
    wide = jnp.concatenate([gram, jnp.zeros((size, LANES - size), F32)], axis=1)
    work = jnp.where(lane < size, wide, jnp.where(lane == row_of + size, 1.0, 0.0))
    pivots = jnp.ones(work.shape, F32)
    for k in range(0, size, BLOCK):
        columns = [jnp.broadcast_to(work[:, c : c + 1], work.shape) for c in range(k, k + BLOCK)]
        tops = [work[c : c + 1, :] for c in range(k, k + BLOCK)]
        for a in range(BLOCK):
            pivot = columns[a][k + a : k + a + 1, :]
            pivots = jnp.where(row_of == k + a, pivot, pivots)
            for c in range(a + 1, BLOCK):
                ratio = columns[c][k + a : k + a + 1, :] / pivot
                columns[c] = columns[c] - columns[a] * ratio
                tops[c] = tops[c] - ratio * tops[a]
            work = work - jnp.where(row_of > k + a, columns[a], 0.0) * (tops[a] / pivot)
    return work / jnp.sqrt(pivots), lane, row_of


def form_basis(inverse, pieces, outs):
    count = len(SWAPS)
    high, low = halves(inverse)
    left = jnp.concatenate([high, low, high], axis=1)
    base = 0
    for piece in range(len(pieces) // count):
        parts = pieces[count * piece : count * piece + count]
        for r in range(parts[0].shape[0]):
            high, low = halves(jnp.concatenate([part[r] for part in parts], axis=0))
            right = jnp.concatenate([high, high, low], axis=0)
            total = jnp.dot(left, right, preferred_element_type=F32)
            for n, out in enumerate(outs):
                out[base + r] = total[8 * n : 8 * n + 8]
        base += parts[0].shape[0]


def basis_of(cells, terms, *refs):
    sums, refs = refs[:terms], refs[terms:]
    count = len(SWAPS)
    pieces, outs, (upper, held) = refs[: -count - 2], refs[-count - 2 : -2], refs[-2:]
    size = sums[0].shape[0]
    gram = functools.reduce(lambda a, b: a + b, [term[...] for term in sums])
    work, lane, row_of = factor(gram / cells, size)
    upper[...] = jnp.where(lane >= row_of, work, 0.0)[:, :size]
    value = work[:, size : 2 * size]
    for _ in range(2):
        value = to_device(value, lax.axis_index("dir"), held).T
    form_basis(value, pieces, outs)


def assemble(spans, *refs):
    parts, (out, held) = refs[:-2], refs[-2:]
    count = len(parts)
    base = 0
    for first, rows in spans:
        share = rows // count
        for k, part in zip(SWAPS, parts):
            at = first + share * (lax.axis_index("dir") ^ k)
            held[pl.ds(at, share)] = part[base : base + share]
        base += share
    for g in range(out.shape[1] // 8):
        out[:, 8 * g : 8 * g + 8, :] = jnp.swapaxes(held[8 * g : 8 * g + 8], 0, 1)


def call(kernel, outs, *args, scratch=(), limit=8, space=pltpu.VMEM):
    vmem = pl.BlockSpec(memory_space=pltpu.VMEM)
    shapes = [
        jax.ShapeDtypeStruct(shape, F32) if isinstance(shape, tuple) else shape for shape in outs
    ]
    return pl.pallas_call(
        kernel,
        out_shape=shapes,
        in_specs=[pl.BlockSpec(memory_space=space)] * len(args),
        out_specs=[vmem] * len(shapes),
        scratch_shapes=[
            pltpu.VMEM(shape, F32) if isinstance(shape, tuple) else shape for shape in scratch
        ],
        compiler_params=pltpu.CompilerParams(vmem_limit_bytes=limit << 20),
    )(*args)


def pairings(count):
    sets = []
    for first in (0, 1):
        pairs = [(i, i + 1) for i in range(first, count - 1, 2)]
        if pairs:
            sets.append(pairs + [(j, i) for i, j in pairs])
    return sets


def swap_bit(value, axis, bit):
    count = lax.axis_size(axis)
    return lax.ppermute(value, axis, [(i, i ^ bit) for i in range(count)])


def partial_sums(value):
    axes = ("gx", "gy", "dir")
    sizes = [lax.axis_size(axis) for axis in axes]
    strides = [sizes[1] * sizes[2], sizes[2], 1]
    bits = [
        [stride << b for b in range(size.bit_length() - 1)] for size, stride in zip(sizes, strides)
    ]
    rest = bits[1][1:] + bits[0]
    stages = [bits[2], bits[1][:1]] + [rest[i : i + 2] for i in range(0, len(rest), 2)]
    count = sizes[0] * strides[0]
    terms = [value]
    for stage in stages:
        value = functools.reduce(lambda a, b: a + b, terms)
        masks = [0]
        for bit in stage:
            masks += [mask | bit for mask in masks]
        terms = [value] + [
            lax.ppermute(value, axes, [(i, i ^ mask) for i in range(count)]) for mask in masks[1:]
        ]
    return terms


def on_device(directions, velocity, viscosity, basal_drag, misfit_weight, ice_mask, grounded):
    own, rows, cols = directions.shape
    across = lax.axis_size("dir")
    args = (directions, velocity, viscosity, basal_drag, misfit_weight, ice_mask, grounded)

    count_y = lax.axis_size("gy")
    sets_x, sets_y = pairings(lax.axis_size("gx")), pairings(count_y)
    counts = (len(sets_x), len(sets_y))
    fields, *messages = call(
        functools.partial(pack, counts),
        [(FIELDS, rows, cols)]
        + [(PLANES + FIELDS, PAD, cols)] * counts[0]
        + [(2, rows // 8, 8, LANES)] * counts[1]
        + [(2, PAD // 8, 8, LANES)] * (counts[0] * counts[1]),
        *args,
        scratch=[pltpu.VMEM(a.shape, a.dtype) for a in args[1:]]
        + [directions.shape]
        + [pltpu.SemaphoreType.DMA((len(args) - 1 + PLANES,))],
        space=pl.ANY,
        limit=60,
    )
    moves = [("gx", s) for s in sets_x] + [("gy", s) for s in sets_y]
    for set_x in sets_x:
        for set_y in sets_y:
            pairs = [(a * count_y + c, b * count_y + d) for a, b in set_x for c, d in set_y]
            moves.append((("gx", "gy"), pairs))
    got = [lax.ppermute(m, axis, pairs) for m, (axis, pairs) in zip(messages, moves)]

    over = REACH + 2
    wide = pl.cdiv(cols + 2 * PAD, SPANS)
    groups = (rows + 2 * PAD) // 8
    lanes_out = pl.cdiv(wide, BANDS) * LANES
    own_lines, places = call(
        line_up,
        [
            (rows, 2 * PLANES, cols),
            jax.ShapeDtypeStruct((BANDS, cols + 2 * LANES, lanes_out), BF16),
        ],
        directions,
        fields,
        limit=24,
    )
    spans = [(0, FIRST_ROWS * rows // 128), (FIRST_ROWS * rows // 128, rows - FIRST_ROWS * rows // 128)]
    pieces = []
    for span in spans:
        tall = span[1] + 2 * over
        high = tall // BANDS
        state = (2, high + 2, wide, 8, LANES)
        own_parts = call(
            functools.partial(solve, counts, span),
            [(span[1] // across, own, cols)] * across,
            *got,
            own_lines,
            places,
            scratch=[
                (2, PLANES + FIELDS, PAD, cols),
                (2, 2, groups, 8, LANES),
                (tall, 8, cols + 2 * LANES),
                (tall, 8, lanes_out),
                (2, high, wide, 8, LANES),
                (3, high, wide, 8, LANES),
                (high, wide, 8, LANES),
                state,
                state,
                state,
            ],
            limit=32,
        )
        pieces.append(
            [own_parts[0]] + [swap_bit(p, "dir", k) for p, k in zip(own_parts[1:], SWAPS[1:])]
        )
    total = own * across
    (gram,) = call(gram_first, [(total, total)], *pieces[0])
    (gram,) = call(
        gram_rest, [(total, total)], gram, *pieces[1], scratch=[(total, total)]
    )
    grams = partial_sums(gram)
    count = rows * cols * lax.axis_size("gx") * lax.axis_size("gy")
    part = (rows // across, own, cols)
    *parts, upper = call(
        functools.partial(basis_of, float(count), len(grams)),
        [part] * across + [(total, total)],
        *grams,
        *pieces[0],
        *pieces[1],
        scratch=[(total, total)],
    )
    parts = [parts[0]] + [swap_bit(p, "dir", k) for p, k in zip(parts[1:], SWAPS[1:])]
    (basis,) = call(
        functools.partial(assemble, spans),
        [(own, rows, cols)],
        *parts,
        scratch=[(rows, own, cols)],
    )
    return (basis, upper)


def solution(mesh):
    tile = P("gx", "gy")
    placed = (P("dir", "gx", "gy"), P(None, "gx", "gy")) + (tile,) * 5
    return jax.shard_map(
        on_device,
        mesh=mesh,
        in_specs=placed,
        out_specs=(P("dir", "gx", "gy"), P()),
        check_vma=False,
    )
```

```python
import functools

import jax
import jax.numpy as jnp
from jax import lax
from jax.experimental import pallas as pl
from jax.experimental.pallas import tpu as pltpu
from jax.sharding import PartitionSpec as P

SWEEPS = 6
damping = 0.8
KEEP_BACK = 1.0 - damping
GROWN, SHRUNK = 1.0 + KEEP_BACK, 1.0 - KEEP_BACK
REACH = 2 * (SWEEPS - 1)
PAD = 16
LANES = 128
BANDS = 4
SPANS = LANES // BANDS
PLANES = 8
SWAPS = (0, 2, 3, 1)
FIELDS = 5
F32 = jnp.float32
BF16 = jnp.bfloat16
WEIGHTS = ((4.0, 1.0), (1.0, 4.0))
BLOCK = 8
PARTS = 2
FIRST_ROWS = 88


def iota(shape, dim):
    return lax.broadcasted_iota(jnp.int32, shape, dim)


def roll(value, shift):
    return pltpu.roll(value, shift % LANES, 1)


def put_fields(out, velocity, viscosity, drag, weight, mask, grounded):
    friction = drag[...] * grounded[...].astype(F32)
    out[0] = friction * velocity[0]
    out[1] = friction * velocity[1]
    out[2] = friction
    out[3] = viscosity[...]
    out[4] = weight[...] * mask[...].astype(F32)


def pack(counts, *refs):
    count_x, count_y = counts
    sources, refs = refs[:7], refs[7:]
    fields, refs = refs[0], refs[1:]
    row_out, refs = refs[:count_x], refs[count_x:]
    col_out, refs = refs[:count_y], refs[count_y:]
    corner_out, refs = refs[: count_x * count_y], refs[count_x * count_y :]
    held, dirs, sems = refs[:6], *refs[6:]
    copies = [
        pltpu.make_async_copy(source, target, sems.at[i])
        for i, (source, target) in enumerate(zip(sources[1:], held))
    ]
    late = [
        pltpu.make_async_copy(sources[0].at[p], dirs.at[p], sems.at[len(copies) + p])
        for p in range(PLANES)
    ]
    for copy in copies + late:
        copy.start()
    for copy in copies:
        copy.wait()
    rows, cols = dirs.shape[1:]
    put_fields(fields, *held)
    for copy in late:
        copy.wait()

    for pairing, out in enumerate(row_out):
        send_last = lax.axis_index("gx") % 2 == pairing
        base = pl.ds(pl.multiple_of(jnp.where(send_last, rows - PAD, 0), PAD), PAD)
        out[:PLANES] = dirs[:, base, :]
        out[PLANES:] = fields[:, base, :]

    lane = iota((8, LANES), 1)
    for g in range(rows // 8):
        span = slice(8 * g, 8 * g + 8)
        for q, (planes, count) in enumerate(((dirs, PLANES), (fields, FIELDS))):
            first = planes[0, span, :LANES]
            last = roll(planes[0, span, cols - LANES :], PAD)
            for p in range(1, count):
                here = lane >= PAD * p
                first = jnp.where(here, roll(planes[p, span, :LANES], PAD * p), first)
                last = jnp.where(
                    here, roll(planes[p, span, cols - LANES :], PAD * (p + 1)), last
                )
            for pairing, out in enumerate(col_out):
                send_last = lax.axis_index("gy") % 2 == pairing
                out[q, g] = jnp.where(send_last, last, first)
    for i in range(count_x):
        send_last = lax.axis_index("gx") % 2 == i
        base = pl.ds(jnp.where(send_last, (rows - PAD) // 8, 0), PAD // 8)
        for j in range(count_y):
            corner_out[i * count_y + j][...] = col_out[j][:, base]


def from_bands(tiles):
    block = iota((8, LANES), 1) // SPANS
    out = []
    for column in range(BANDS):
        value = tiles[0]
        for band in range(1, BANDS):
            value = jnp.where(block == (column + band) % BANDS, tiles[band], value)
        out.append(roll(value, -SPANS * column) if column else value)
    return out


def to_bands(tiles):
    block = iota((8, LANES), 1) // SPANS
    turned = [roll(tile, SPANS * column) if column else tile for column, tile in enumerate(tiles)]
    out = []
    for band in range(BANDS):
        value = turned[0]
        for column in range(1, BANDS):
            value = jnp.where(block == (column + band) % BANDS, turned[column], value)
        out.append(value)
    return out


def line_up(dirs, fields, lines, places):
    rows, cols = dirs.shape[1:]
    for g in range(rows // 8):
        at = slice(8 * g, 8 * g + 8)
        lines[at, :PLANES, :] = jnp.swapaxes(dirs[:, at, :], 0, 1)
        stack = [fields[k, at, :] for k in range(FIELDS)]
        stack += [jnp.zeros((8, cols), F32)] * (PLANES - FIELDS)
        lines[at, PLANES:, :] = jnp.swapaxes(jnp.stack(stack), 0, 1)
    wide = pl.cdiv(cols + 2 * PAD, SPANS)
    k, lane = (iota(places.shape[1:], dim) for dim in (0, 1))
    slot = k % PAD + jnp.where(k < cols + LANES, 0, cols + PAD)
    column = jnp.where(k < cols, k + PAD, slot)
    tile, block, span = lane // LANES, (lane // SPANS) % BANDS, lane % SPANS
    for band in range(BANDS):
        j = BANDS * tile + (block + BANDS - band) % BANDS
        here = (column == wide * span + j) & (j < wide)
        places[band] = jnp.where(here, 1.0, 0.0).astype(BF16)


def split_dot(value, places, transposed=False):
    total = None
    for step in range(PARTS):
        part = value.astype(BF16)
        product = lax.dot_general(
            part,
            places,
            (((1,), (1 if transposed else 0,)), ((), ())),
            preferred_element_type=F32,
        )
        total = product if total is None else total + product
        if step < PARTS - 1:
            value = value - part.astype(F32)
    return total


def solve(counts, span, *refs):
    count_x, count_y = counts
    row_first, row_count = span
    got_rows, refs = refs[:count_x], refs[count_x:]
    got_cols, refs = refs[:count_y], refs[count_y:]
    got_corners, refs = refs[: count_x * count_y], refs[count_x * count_y :]
    own_lines, places, *refs = refs
    *outs, halo_rows, halo_cols, lined, turned, planes, coeffs, extras, base, ping, pong = refs
    rows, _, cols = own_lines.shape
    tall = lined.shape[0]
    over = (tall - row_count) // 2
    high = tall // BANDS
    wide = planes.shape[2]
    groups = (rows + 2 * PAD) // 8
    edge = PAD // 8
    even = [lax.axis_index("gx") % 2 == 0, lax.axis_index("gy") % 2 == 0]

    def sides(axis, one, two):
        return jnp.where(even[axis], two, one), jnp.where(even[axis], one, two)

    def pair(got, index):
        one = got[0][index]
        return one, (got[1][index] if len(got) > 1 else jnp.zeros_like(one))

    for p in range(PLANES + FIELDS):
        halo_rows[0, p], halo_rows[1, p] = sides(0, *pair(got_rows, p))
    for q in range(2):
        left, right = sides(1, *pair(got_cols, q))
        halo_cols[0, q, edge : groups - edge] = left
        halo_cols[1, q, edge : groups - edge] = right
        by_x = [
            sides(1, *pair(got_corners[i * count_y : (i + 1) * count_y], q))
            for i in range(count_x)
        ]
        for side in range(2):
            one = by_x[0][side]
            two = by_x[1][side] if count_x > 1 else jnp.zeros_like(one)
            above, below = sides(0, one, two)
            halo_cols[side, q, :edge] = above
            halo_cols[side, q, groups - edge :] = below

    lanes_out = turned.shape[2]
    lane = iota((8, LANES), 1)
    own_slot = lane // PAD == iota((8, LANES), 0)

    def over_rows(body):
        for i in range(high):
            body(i)

    for q, (first, count) in enumerate(((0, PLANES), (PLANES, FIELDS))):
        for g in range(groups):
            lines_of = [8 * g + d - PAD - (row_first - over) for d in range(8)]
            if lines_of[-1] < 0 or lines_of[0] >= tall:
                continue
            inner = edge <= g < groups - edge
            if not inner:
                side, at = (0, g) if g < edge else (1, g - groups + edge)
                stack = [
                    halo_rows[side, first + p, 8 * at : 8 * at + 8, :] for p in range(count)
                ]
                stack += [jnp.zeros((8, cols), F32)] * (PLANES - count)
                lines = jnp.swapaxes(jnp.stack(stack), 0, 1)
            for d, line in enumerate(lines_of):
                if 0 <= line < tall:
                    lined[line, :, :cols] = (
                        own_lines[8 * (g - edge) + d, PLANES * q : PLANES * q + PLANES, :]
                        if inner
                        else lines[d]
                    )
                    for side_y in range(2):
                        begin = cols + LANES * side_y
                        lined[line, :, begin : begin + LANES] = jnp.where(
                            own_slot, halo_cols[side_y, q, g, d : d + 1, :], 0.0
                        )

        for b in range(BANDS):
            value = lined[pl.ds(high * b, high)].reshape(high * 8, cols + 2 * LANES)
            turned[pl.ds(high * b, high)] = split_dot(value, places[b]).reshape(
                high, 8, lanes_out
            )

        def band(i):
            for t in range(lanes_out // LANES):
                tiles = [
                    turned[high * b + i, :, LANES * t : LANES * t + LANES] for b in range(BANDS)
                ]
                for j, tile in enumerate(from_bands(tiles)[: wide - BANDS * t], BANDS * t):
                    planes[q, i, j] = tile

        over_rows(band)

    row_of = iota((8, LANES), 0)
    kind = row_of % 4
    ax = jnp.where(row_of < 4, WEIGHTS[0][0], WEIGHTS[1][0])
    ay = jnp.where(row_of < 4, WEIGHTS[0][1], WEIGHTS[1][1])
    along = jnp.where(kind < 2, ax, ay)

    def weigh(i, above, below, turn_above, turn_below):
        def field(k, row, j):
            return jnp.broadcast_to(planes[1, row, j, k : k + 1, :], (8, LANES))

        mids = [field(3, i, j) for j in range(wide)]
        wests = [roll(mids[-1], 1)] + mids[:-1]
        easts = mids[1:] + [roll(mids[0], -1)]
        for j in range(wide):
            mid = mids[j]
            up, down = field(3, above, j), field(3, below, j)
            up = roll(up, SPANS) if turn_above else up
            down = roll(down, -SPANS) if turn_below else down
            east, west = 0.5 * (mid + down), 0.5 * (mid + up)
            north, south = 0.5 * (mid + easts[j]), 0.5 * (mid + wests[j])
            along_x, along_y = east + west, north + south
            friction, kept = field(2, i, j), field(4, i, j)

            diagonal = ax * along_x + ay * along_y + friction
            gain = jnp.where(kept != 0.0, damping / diagonal, 0.0)
            face = jnp.where(
                kind < 2,
                jnp.where(kind == 0, east, west),
                jnp.where(kind == 2, north, south),
            )
            weight = gain * along * face
            coeffs[0, i, j] = weight * (1.0 / GROWN)
            coeffs[1, i, j] = weight * (1.0 / KEEP_BACK)
            coeffs[2, i, j] = weight * (-1.0 / SHRUNK)
            pull = jnp.where(row_of < 4, field(0, i, j), field(1, i, j))
            extras[i, j] = jnp.where(
                kind == 1,
                GROWN * gain * kept,
                jnp.where(kind == 0, gain, GROWN) * -pull,
            )

    weigh(0, high - 1, 1, True, False)
    weigh(high - 1, high - 2, 0, False, True)

    def weigh_inner(i, _):
        weigh(i, i - 1, i + 1, False, False)
        return 0

    lax.fori_loop(1, high - 1, weigh_inner, 0, unroll=2)

    def put(ref, m, i, j, value, edges=True):
        ref[m, i + 1, j] = value
        if edges and isinstance(i, int):
            if i == 0:
                ref[m, high + 1, j] = roll(value, -SPANS)
            if i == high - 1:
                ref[m, 0, j] = roll(value, SPANS)

    def extra(kind, m, i, j):
        return extras[i, j, pl.ds(4 * m + kind, 1), :]

    def start(i):
        for j in range(wide):
            for m in range(2):
                put(base, m, i, j, extra(0, m, i, j) * planes[0, i, j])

    over_rows(start)

    def sweep(source, scale, store):
        for m in range(2):
            above, mids = ([source[m, i, j] for j in range(wide)] for i in range(2))
            for i in range(high):
                below = [source[m, i + 2, j] for j in range(wide)]
                before = [roll(mids[-1], 1)] + mids[:-1]
                after = mids[1:] + [roll(mids[0], -1)]
                for j in range(wide):
                    e, w, n, s = (
                        coeffs[scale, i, j, 4 * m + d : 4 * m + d + 1, :] for d in range(4)
                    )
                    along_x = e * below[j] + w * above[j]
                    along_y = n * after[j] + s * before[j]
                    store(m, i, j, mids[j] + (along_x + along_y))
                above, mids = mids, below

    def to(ref):
        return lambda m, i, j, value: put(ref, m, i, j, value)

    def solve_from_base(kind, _):
        sweep(base, 0, to(ping))
        sweep(ping, 1, to(pong))

        def add(m, i, j, value):
            put(base, m, i, j, ping[m, i + 1, j] + (KEEP_BACK * GROWN) * value)

        sweep(pong, 0, add)
        sweep(base, 1, to(pong))

        def last(m, i, j, value):
            value = base[m, i + 1, j] - (KEEP_BACK * SHRUNK) * value
            put(base, m, i, j, extra(kind, m, i, j) * value)

        sweep(pong, 2, last)
        return 0

    lax.fori_loop(1, 3, solve_from_base, 0)

    def unband(i):
        for t in range(lanes_out // LANES):
            columns = range(BANDS * t, min(BANDS * t + BANDS, wide))
            tiles = [base[0, i + 1, j] + base[1, i + 1, j] for j in columns]
            tiles += [jnp.zeros((8, LANES), F32)] * (BANDS - len(tiles))
            for b, tile in enumerate(to_bands(tiles)):
                turned[high * b + i, :, LANES * t : LANES * t + LANES] = tile

    over_rows(unband)

    for b in range(BANDS):
        value = turned[pl.ds(high * b, high)].reshape(high * 8, lanes_out)
        value = split_dot(value, places[b, :cols, :], transposed=True)
        lined[pl.ds(high * b, high), :, :cols] = value.reshape(high, 8, cols)

    part = row_count // len(outs)
    for k, out in zip(SWAPS, outs):
        out[...] = lined[pl.ds(over + part * (lax.axis_index("dir") ^ k), part), :, :cols]


def halves(value):
    high = value.astype(BF16)
    return high, (value - high.astype(F32)).astype(BF16)


def gram_sum(parts):
    total = cross = None
    dims = (((1,), (1,)), ((), ()))
    for r in range(parts[0].shape[0]):
        high, low = halves(jnp.concatenate([part[r] for part in parts], axis=0))
        one = lax.dot_general(high, high, dims, preferred_element_type=F32)
        two = lax.dot_general(high, low, dims, preferred_element_type=F32)
        total = one if total is None else total + one
        cross = two if cross is None else cross + two
    return total + (cross + cross.T)


def gram_first(*refs):
    refs[-1][...] = gram_sum(refs[:-1])


def by_device(value, me, held):
    for n, k in enumerate(SWAPS):
        held[pl.ds(pl.multiple_of(8 * (me ^ k), 8), 8), :] = value[8 * n : 8 * n + 8]
    return held[...]


def to_device(value, me, held):
    held[...] = value
    blocks = [held[pl.ds(pl.multiple_of(8 * (me ^ k), 8), 8), :] for k in SWAPS]
    return jnp.concatenate(blocks, axis=0)


def gram_rest(before, *refs):
    parts, (gram, held) = refs[:-2], refs[-2:]
    total = before[...] + gram_sum(parts)
    for _ in range(2):
        total = by_device(total, lax.axis_index("dir"), held).T
    gram[...] = total


def factor(gram, size):
    lane = iota((size, LANES), 1)
    row_of = iota((size, LANES), 0)
    wide = jnp.concatenate([gram, jnp.zeros((size, LANES - size), F32)], axis=1)
    work = jnp.where(lane < size, wide, jnp.where(lane == row_of + size, 1.0, 0.0))
    pivots = jnp.ones(work.shape, F32)
    for k in range(0, size, BLOCK):
        columns = [jnp.broadcast_to(work[:, c : c + 1], work.shape) for c in range(k, k + BLOCK)]
        tops = [work[c : c + 1, :] for c in range(k, k + BLOCK)]
        for a in range(BLOCK):
            pivot = columns[a][k + a : k + a + 1, :]
            pivots = jnp.where(row_of == k + a, pivot, pivots)
            for c in range(a + 1, BLOCK):
                ratio = columns[c][k + a : k + a + 1, :] / pivot
                columns[c] = columns[c] - columns[a] * ratio
                tops[c] = tops[c] - ratio * tops[a]
            work = work - jnp.where(row_of > k + a, columns[a], 0.0) * (tops[a] / pivot)
    return work / jnp.sqrt(pivots), lane, row_of


def form_basis(inverse, pieces, outs):
    count = len(SWAPS)
    high, low = halves(inverse)
    left = jnp.concatenate([high, low, high], axis=1)
    base = 0
    for piece in range(len(pieces) // count):
        parts = pieces[count * piece : count * piece + count]
        for r in range(parts[0].shape[0]):
            high, low = halves(jnp.concatenate([part[r] for part in parts], axis=0))
            right = jnp.concatenate([high, high, low], axis=0)
            total = jnp.dot(left, right, preferred_element_type=F32)
            for n, out in enumerate(outs):
                out[base + r] = total[8 * n : 8 * n + 8]
        base += parts[0].shape[0]


def basis_of(cells, terms, *refs):
    sums, refs = refs[:terms], refs[terms:]
    count = len(SWAPS)
    pieces, outs, (upper, held) = refs[: -count - 2], refs[-count - 2 : -2], refs[-2:]
    size = sums[0].shape[0]
    gram = functools.reduce(lambda a, b: a + b, [term[...] for term in sums])
    work, lane, row_of = factor(gram / cells, size)
    upper[...] = jnp.where(lane >= row_of, work, 0.0)[:, :size]
    value = work[:, size : 2 * size]
    for _ in range(2):
        value = to_device(value, lax.axis_index("dir"), held).T
    form_basis(value, pieces, outs)


def assemble(spans, *refs):
    parts, (out, held, turned, sems) = refs[:-4], refs[-4:]
    count = len(parts)
    base = 0
    for first, rows in spans:
        share = rows // count
        for k, part in zip(SWAPS, parts):
            at = first + share * (lax.axis_index("dir") ^ k)
            held[pl.ds(at, share)] = part[base : base + share]
        base += share
    copies = []
    chunk = out.shape[1] // sems.shape[0]
    for c in range(sems.shape[0]):
        at = slice(chunk * c, chunk * c + chunk)
        for g in range(chunk * c // 8, (chunk * c + chunk) // 8):
            turned[:, 8 * g : 8 * g + 8, :] = jnp.swapaxes(held[8 * g : 8 * g + 8], 0, 1)
        copies.append(pltpu.make_async_copy(turned.at[:, at, :], out.at[:, at, :], sems.at[c]))
        copies[-1].start()
    for copy in copies:
        copy.wait()


def call(kernel, outs, *args, scratch=(), limit=8, space=pltpu.VMEM, out_space=pltpu.VMEM):
    shapes = [
        jax.ShapeDtypeStruct(shape, F32) if isinstance(shape, tuple) else shape for shape in outs
    ]
    return pl.pallas_call(
        kernel,
        out_shape=shapes,
        in_specs=[pl.BlockSpec(memory_space=space)] * len(args),
        out_specs=[pl.BlockSpec(memory_space=out_space)] * len(shapes),
        scratch_shapes=[
            pltpu.VMEM(shape, F32) if isinstance(shape, tuple) else shape for shape in scratch
        ],
        compiler_params=pltpu.CompilerParams(vmem_limit_bytes=limit << 20),
    )(*args)


def pairings(count):
    sets = []
    for first in (0, 1):
        pairs = [(i, i + 1) for i in range(first, count - 1, 2)]
        if pairs:
            sets.append(pairs + [(j, i) for i, j in pairs])
    return sets


def swap_bit(value, axis, bit):
    count = lax.axis_size(axis)
    return lax.ppermute(value, axis, [(i, i ^ bit) for i in range(count)])


def partial_sums(value):
    axes = ("gx", "gy", "dir")
    sizes = [lax.axis_size(axis) for axis in axes]
    strides = [sizes[1] * sizes[2], sizes[2], 1]
    bits = [
        [stride << b for b in range(size.bit_length() - 1)] for size, stride in zip(sizes, strides)
    ]
    rest = bits[1][1:] + bits[0]
    stages = [bits[2], bits[1][:1]] + [rest[i : i + 2] for i in range(0, len(rest), 2)]
    count = sizes[0] * strides[0]
    terms = [value]
    for stage in stages:
        value = functools.reduce(lambda a, b: a + b, terms)
        masks = [0]
        for bit in stage:
            masks += [mask | bit for mask in masks]
        terms = [value] + [
            lax.ppermute(value, axes, [(i, i ^ mask) for i in range(count)]) for mask in masks[1:]
        ]
    return terms


def on_device(directions, velocity, viscosity, basal_drag, misfit_weight, ice_mask, grounded):
    own, rows, cols = directions.shape
    across = lax.axis_size("dir")
    args = (directions, velocity, viscosity, basal_drag, misfit_weight, ice_mask, grounded)

    count_y = lax.axis_size("gy")
    sets_x, sets_y = pairings(lax.axis_size("gx")), pairings(count_y)
    counts = (len(sets_x), len(sets_y))
    fields, *messages = call(
        functools.partial(pack, counts),
        [(FIELDS, rows, cols)]
        + [(PLANES + FIELDS, PAD, cols)] * counts[0]
        + [(2, rows // 8, 8, LANES)] * counts[1]
        + [(2, PAD // 8, 8, LANES)] * (counts[0] * counts[1]),
        *args,
        scratch=[pltpu.VMEM(a.shape, a.dtype) for a in args[1:]]
        + [directions.shape]
        + [pltpu.SemaphoreType.DMA((len(args) - 1 + PLANES,))],
        space=pl.ANY,
        limit=60,
    )
    moves = [("gx", s) for s in sets_x] + [("gy", s) for s in sets_y]
    for set_x in sets_x:
        for set_y in sets_y:
            pairs = [(a * count_y + c, b * count_y + d) for a, b in set_x for c, d in set_y]
            moves.append((("gx", "gy"), pairs))
    got = [lax.ppermute(m, axis, pairs) for m, (axis, pairs) in zip(messages, moves)]

    over = REACH + 2
    wide = pl.cdiv(cols + 2 * PAD, SPANS)
    groups = (rows + 2 * PAD) // 8
    lanes_out = pl.cdiv(wide, BANDS) * LANES
    own_lines, places = call(
        line_up,
        [
            (rows, 2 * PLANES, cols),
            jax.ShapeDtypeStruct((BANDS, cols + 2 * LANES, lanes_out), BF16),
        ],
        directions,
        fields,
        limit=24,
    )
    spans = [(0, FIRST_ROWS * rows // 128), (FIRST_ROWS * rows // 128, rows - FIRST_ROWS * rows // 128)]
    pieces = []
    for span in spans:
        tall = span[1] + 2 * over
        high = tall // BANDS
        state = (2, high + 2, wide, 8, LANES)
        own_parts = call(
            functools.partial(solve, counts, span),
            [(span[1] // across, own, cols)] * across,
            *got,
            own_lines,
            places,
            scratch=[
                (2, PLANES + FIELDS, PAD, cols),
                (2, 2, groups, 8, LANES),
                (tall, 8, cols + 2 * LANES),
                (tall, 8, lanes_out),
                (2, high, wide, 8, LANES),
                (3, high, wide, 8, LANES),
                (high, wide, 8, LANES),
                state,
                state,
                state,
            ],
            limit=32,
        )
        pieces.append(
            [own_parts[0]] + [swap_bit(p, "dir", k) for p, k in zip(own_parts[1:], SWAPS[1:])]
        )
    total = own * across
    (gram,) = call(gram_first, [(total, total)], *pieces[0])
    (gram,) = call(
        gram_rest, [(total, total)], gram, *pieces[1], scratch=[(total, total)]
    )
    grams = partial_sums(gram)
    count = rows * cols * lax.axis_size("gx") * lax.axis_size("gy")
    part = (rows // across, own, cols)
    *parts, upper = call(
        functools.partial(basis_of, float(count), len(grams)),
        [part] * across + [(total, total)],
        *grams,
        *pieces[0],
        *pieces[1],
        scratch=[(total, total)],
    )
    parts = [parts[0]] + [swap_bit(p, "dir", k) for p, k in zip(parts[1:], SWAPS[1:])]
    (basis,) = call(
        functools.partial(assemble, spans),
        [(own, rows, cols)],
        *parts,
        scratch=[(rows, own, cols), (own, rows, cols), pltpu.SemaphoreType.DMA((4,))],
        out_space=pltpu.HBM,
    )
    return (basis, upper)


def solution(mesh):
    tile = P("gx", "gy")
    placed = (P("dir", "gx", "gy"), P(None, "gx", "gy")) + (tile,) * 5
    return jax.shard_map(
        on_device,
        mesh=mesh,
        in_specs=placed,
        out_specs=(P("dir", "gx", "gy"), P()),
        check_vma=False,
    )
```
